32 devices in a mesh: seq: 8 (over z, x), rep: 4 (over y, core).
Axes of the slice: x: 2, y: 2, z: 4, core: 2. Of those that a mesh axis runs over, the one named last changes fastest.
Arguments:
- t_query: bfloat16 [4, 1024, 4096], P('rep', 'seq'), may hold values from -45 to 45
- t_key: bfloat16 [4, 1024, 512], P('rep', 'seq'), may hold values from -4 to 4
- t_value: bfloat16 [4, 1024, 512], P('rep', 'seq'), may hold values from -6 to 6
- s_query: bfloat16 [4, 1024, 2048], P('rep', 'seq'), may hold values from -45 to 45
- s_key: bfloat16 [4, 1024, 512], P('rep', 'seq'), may hold values from -4 to 4
- student_value: bfloat16 [4, 1024, 512], P('rep', 'seq'), may hold values from -6 to 6
- student_wo: bfloat16 [2048, 2048], P('seq'), may hold values from -0.125 to 0.125
- projection: bfloat16 [4096, 2048], P('seq'), may hold values from -0.09375 to 0.09375
- doc_ids: int32 [4, 1024], P('rep'), may hold values from 0 to 15, never falling along the last dimension, each value on 1 to 256 neighbouring positions
- span_order: int32 [4, 16], P('rep'), may hold values from 0 to 15, each once within a row
Outputs:
- seq_loss: float32 [4], P('rep')
- d_wo: float32 [2048, 2048], P('seq', 'rep')
- d_query: bfloat16 [4, 1024, 2048], P('rep', 'seq')
- d_key: bfloat16 [4, 1024, 512], P('rep', 'seq')
- d_value: bfloat16 [4, 1024, 512], P('rep', 'seq')
The draws below stay inside these ranges and needn't reach their ends.
All inputs are finite; a program needn't handle non-finite values.
Results may differ from the reference program's by a relative error of at most 0.018.
The reference program's roundings to bfloat16 on the way count: a program that leaves them out, or rounds other values in their place, can miss the bound.
Values may be sent and summed in bfloat16 or wider, within the bound.
A program may use at most 128 MiB of HBM per device.

```python
import math
import jax
import jax.numpy as jnp
import numpy as np
from jax import lax

HEAD_WIDTH = 128
TQH = 32
TKV = 4
STUDENT_QUERIES = 16
STUDENT_KEYS = 4
DS = 2048
DOCS = 16
SEQUENCE_LENGTH = 1024
HALVES = 16
SEQUENCE_COUNT = 4
N_SEQ = 8


def matched_couple(key, q_heads, kv_heads):
    base_key = jax.random.fold_in(key, 7)
    shape_q = (SEQUENCE_COUNT, SEQUENCE_LENGTH // 8, 8, q_heads, HEAD_WIDTH)
    shape_k = (SEQUENCE_COUNT, SEQUENCE_LENGTH // 8, 8, kv_heads, HEAD_WIDTH)
    key_vals = jnp.clip(jax.random.normal(jax.random.fold_in(base_key, 1), shape_k, jnp.float32), -4.0, 4.0)
    query_vals = jnp.clip(jax.random.normal(jax.random.fold_in(base_key, 3), shape_q, jnp.float32), -4.0, 4.0)
    return (query_vals.reshape(SEQUENCE_COUNT, SEQUENCE_LENGTH, q_heads * HEAD_WIDTH), key_vals.reshape(SEQUENCE_COUNT, SEQUENCE_LENGTH, kv_heads * HEAD_WIDTH))


def draw_t_query(key, part):
    return matched_couple(jax.random.fold_in(key, 11), TQH, TKV)[0].astype(jnp.bfloat16)


def draw_t_key(key, part):
    return matched_couple(jax.random.fold_in(key, 11), TQH, TKV)[1].astype(jnp.bfloat16)


def draw_s_query(key, part):
    return matched_couple(jax.random.fold_in(key, 12), STUDENT_QUERIES, STUDENT_KEYS)[0].astype(jnp.bfloat16)


def draw_s_key(key, part):
    return matched_couple(jax.random.fold_in(key, 12), STUDENT_QUERIES, STUDENT_KEYS)[1].astype(jnp.bfloat16)


def block_levels(key, extent, pieces, least, top_value):
    loudness, own = 1.0, jax.random.fold_in(key, 6)
    for axis_at, shards_of in pieces:
        heights = jnp.exp(jax.random.uniform(jax.random.fold_in(own, axis_at), (shards_of,), jnp.float32, least / len(pieces), top_value / len(pieces)))
        loudness = loudness * jnp.repeat(heights, extent[axis_at] // shards_of).reshape([-1 if axis == axis_at else 1 for axis in range(len(extent))])
    return loudness


def profile(count, total, most, lean):
    weights = [(1 << 20) // math.isqrt(standing ** lean) + 1 for standing in range(2, count + 1)]
    surplus, given = total - most - (count - 1), [1] * (count - 1)
    while surplus > 0:
        movable = [i for i in range(count - 1) if given[i] < most]
        whole, budget = sum([weights[i] for i in movable]), surplus
        for i in movable:
            extra = min(most - given[i], max(1, budget * weights[i] // whole), surplus)
            given[i] = given[i] + extra
            surplus = surplus - extra
    return np.array([most] + given)


def ragged(own_key, amount, total, most, skew):
    if amount == 2:
        one = jax.random.randint(own_key, (), max(1, total - most), min(most, total - 1) + 1)
        return jnp.stack([one, total - one])
    lengths = jnp.asarray(profile(amount, total, most, skew), jnp.int32)
    twos = (amount - 1) // 2
    source_of, taker = lengths[1:1 + 2 * twos:2], lengths[2:2 + 2 * twos:2]
    margin = jnp.minimum(source_of - 1, most - taker)
    moved = jax.random.randint(jax.random.fold_in(own_key, 1), (twos,), 0, 1 << 20) % (margin + 1)
    lengths = lengths.at[1:1 + 2 * twos:2].set(source_of - moved).at[2:2 + 2 * twos:2].set(taker + moved)
    return lengths[jax.random.permutation(jax.random.fold_in(own_key, 2), amount)]


def normal_values(key, shape, spread, most, cuts=(), held_as=jnp.bfloat16):
    values = spread * jax.random.normal(key, shape, jnp.float32)
    if cuts:
        values = values * block_levels(key, shape, cuts, -0.22, 0.18)
    return jnp.clip(values, -most, most).astype(held_as)


def setup_inputs(seed: int = 0) -> dict:
    arg_keys = jax.random.split(jax.random.key(seed), 11)
    t_query = draw_t_query(jax.random.fold_in(arg_keys[10], 71), 0)
    t_key = draw_t_key(jax.random.fold_in(arg_keys[10], 71), 0)
    t_value = normal_values(arg_keys[2], (SEQUENCE_COUNT, SEQUENCE_LENGTH, TKV * HEAD_WIDTH), 1.0, 6.0, ((0, 4), (1, 8)))
    s_query = draw_s_query(jax.random.fold_in(arg_keys[10], 71), 0)
    s_key = draw_s_key(jax.random.fold_in(arg_keys[10], 71), 0)
    student_value = normal_values(arg_keys[5], (SEQUENCE_COUNT, SEQUENCE_LENGTH, STUDENT_KEYS * HEAD_WIDTH), 1.0, 6.0, ((0, 4), (1, 8)))
    student_wo = normal_values(arg_keys[6], (STUDENT_QUERIES * HEAD_WIDTH, DS), (STUDENT_QUERIES * HEAD_WIDTH) ** -0.5, 0.125, ((0, 8),))
    projection = normal_values(arg_keys[7], (TQH * HEAD_WIDTH, DS), (TQH * HEAD_WIDTH) ** -0.5, 0.09375, ((0, 8),))
    doc_ids = jax.vmap(lambda own: jnp.searchsorted(jnp.cumsum(ragged(own, DOCS, SEQUENCE_LENGTH, SEQUENCE_LENGTH // 4, 2)), jnp.arange(SEQUENCE_LENGTH), side="right"))(jax.random.split(arg_keys[8], SEQUENCE_COUNT)).reshape((SEQUENCE_COUNT, SEQUENCE_LENGTH)).astype(jnp.int32)
    span_order = jax.vmap(lambda own: jax.random.permutation(own, HALVES))(jax.random.split(arg_keys[9], SEQUENCE_COUNT)).reshape((SEQUENCE_COUNT, HALVES)).astype(jnp.int32)
    return dict(t_query=t_query, t_key=t_key, t_value=t_value, s_query=s_query, s_key=s_key, student_value=student_value, student_wo=student_wo, projection=projection, doc_ids=doc_ids, span_order=span_order)


MASKED = -1e+30

def stored_positions(order_row):
    half_len = SEQUENCE_LENGTH // HALVES
    offsets = jnp.arange(half_len, dtype=jnp.int32)
    return (order_row[:, None].astype(jnp.int32) * half_len + offsets[None, :]).reshape(SEQUENCE_LENGTH)

def soft_rows(scores, allowed):
    scores = jnp.where(allowed, scores, MASKED)
    maximum = lax.optimization_barrier(jnp.max(scores, axis=1, keepdims=True))
    weights = jnp.where(allowed, jnp.exp(scores - maximum), 0.0)
    return (weights, lax.optimization_barrier(jnp.sum(weights, axis=1, keepdims=True)))

def group_sums(parts):
    per_group = parts.reshape(N_SEQ, STUDENT_QUERIES // N_SEQ, SEQUENCE_LENGTH, HEAD_WIDTH).sum(axis=1)
    rounded_result = lax.optimization_barrier(per_group.astype(jnp.bfloat16)).astype(jnp.float32)
    each_head_part = rounded_result.reshape(STUDENT_KEYS, N_SEQ // STUDENT_KEYS, SEQUENCE_LENGTH, HEAD_WIDTH).sum(axis=1).astype(jnp.bfloat16)
    return jnp.transpose(each_head_part, (1, 0, 2)).reshape(SEQUENCE_LENGTH, STUDENT_KEYS * HEAD_WIDTH)

def one_sequence(t_query, t_key, t_value, s_query, s_key, student_value, doc_row, order_row, student_wo, projection):
    scaling = 1.0 / math.sqrt(HEAD_WIDTH)
    positions = stored_positions(order_row)
    stored_docs = jnp.take(doc_row, positions)
    allowed = (stored_docs[:, None] == stored_docs[None, :]) & (positions[None, :] <= positions[:, None])
    teacher_share = TQH // TKV
    student_portion = STUDENT_QUERIES // STUDENT_KEYS

    def teacher_head(head_id):
        group_id = head_id // teacher_share
        queries = lax.dynamic_slice_in_dim(t_query, head_id * HEAD_WIDTH, HEAD_WIDTH, 1)
        key_rows = lax.dynamic_slice_in_dim(t_key, group_id * HEAD_WIDTH, HEAD_WIDTH, 1)
        val_rows = lax.dynamic_slice_in_dim(t_value, group_id * HEAD_WIDTH, HEAD_WIDTH, 1)
        scores = jnp.dot(queries, key_rows.T, preferred_element_type=jnp.float32) * scaling
        weights, totals = soft_rows(scores, allowed)
        mixed_rows = jnp.dot(weights.astype(jnp.bfloat16), val_rows, preferred_element_type=jnp.float32) / totals
        return mixed_rows.astype(jnp.bfloat16)
    teacher_ids = jnp.arange(TQH, dtype=jnp.int32)
    teacher_out = jnp.transpose(lax.map(teacher_head, teacher_ids), (1, 0, 2)).reshape(SEQUENCE_LENGTH, TQH * HEAD_WIDTH)

    def student_head(head_id):
        group_id = head_id // student_portion
        queries = lax.dynamic_slice_in_dim(s_query, head_id * HEAD_WIDTH, HEAD_WIDTH, 1)
        key_rows = lax.dynamic_slice_in_dim(s_key, group_id * HEAD_WIDTH, HEAD_WIDTH, 1)
        val_rows = lax.dynamic_slice_in_dim(student_value, group_id * HEAD_WIDTH, HEAD_WIDTH, 1)
        scores = jnp.dot(queries, key_rows.T, preferred_element_type=jnp.float32) * scaling
        weights, totals = soft_rows(scores, allowed)
        probs_h = (weights / totals).astype(jnp.bfloat16)
        mixed_rows = jnp.dot(probs_h, val_rows, preferred_element_type=jnp.float32).astype(jnp.bfloat16)
        return (probs_h, mixed_rows)
    student_ids = jnp.arange(STUDENT_QUERIES, dtype=jnp.int32)
    student_probs, student_heads = lax.map(student_head, student_ids)
    student_out = jnp.transpose(student_heads, (1, 0, 2)).reshape(SEQUENCE_LENGTH, STUDENT_QUERIES * HEAD_WIDTH)
    width_s = STUDENT_QUERIES // N_SEQ * HEAD_WIDTH
    width_t = TQH // N_SEQ * HEAD_WIDTH

    def add_group(running, group_id):
        student_part = lax.dynamic_slice_in_dim(student_out, group_id * width_s, width_s, 1)
        wo_part = lax.dynamic_slice_in_dim(student_wo, group_id * width_s, width_s, 0)
        teacher_part = lax.dynamic_slice_in_dim(teacher_out, group_id * width_t, width_t, 1)
        proj_part = lax.dynamic_slice_in_dim(projection, group_id * width_t, width_t, 0)
        term = jnp.dot(student_part, wo_part, preferred_element_type=jnp.float32) - jnp.dot(teacher_part, proj_part, preferred_element_type=jnp.float32)
        rounded_result = lax.optimization_barrier(term.astype(jnp.bfloat16))
        return (running + rounded_result.astype(jnp.float32), None)
    diff, unused = lax.scan(add_group, jnp.zeros((SEQUENCE_LENGTH, DS), jnp.float32), jnp.arange(N_SEQ, dtype=jnp.int32))
    seq_loss = jnp.sum(diff * diff) / (SEQUENCE_LENGTH * DS)
    grad_out = diff.astype(jnp.bfloat16)
    d_attn = jnp.dot(grad_out, student_wo.T, preferred_element_type=jnp.float32).astype(jnp.bfloat16)
    d_weight = jnp.dot(student_out.T, grad_out, preferred_element_type=jnp.float32)

    def student_back(items):
        head_id, probs_h, out_h = items
        group_id = head_id // student_portion
        queries = lax.dynamic_slice_in_dim(s_query, head_id * HEAD_WIDTH, HEAD_WIDTH, 1)
        key_rows = lax.dynamic_slice_in_dim(s_key, group_id * HEAD_WIDTH, HEAD_WIDTH, 1)
        val_rows = lax.dynamic_slice_in_dim(student_value, group_id * HEAD_WIDTH, HEAD_WIDTH, 1)
        grad_h = lax.dynamic_slice_in_dim(d_attn, head_id * HEAD_WIDTH, HEAD_WIDTH, 1)
        row_delta = lax.optimization_barrier(jnp.sum(grad_h.astype(jnp.float32) * out_h.astype(jnp.float32), axis=1, keepdims=True))
        d_prob = jnp.dot(grad_h, val_rows.T, preferred_element_type=jnp.float32)
        d_score = (probs_h.astype(jnp.float32) * (d_prob - row_delta)).astype(jnp.bfloat16)
        d_query = (jnp.dot(d_score, key_rows, preferred_element_type=jnp.float32) * scaling).astype(jnp.bfloat16)
        d_key = jnp.dot(d_score.T, queries, preferred_element_type=jnp.float32) * scaling
        d_value = jnp.dot(probs_h.T, grad_h, preferred_element_type=jnp.float32)
        return (d_query, d_key, d_value)
    d_query, d_key, d_value = lax.map(student_back, (student_ids, student_probs, student_heads))
    d_query = jnp.transpose(d_query, (1, 0, 2)).reshape(SEQUENCE_LENGTH, STUDENT_QUERIES * HEAD_WIDTH)
    return (seq_loss, d_weight, d_query, group_sums(d_key), group_sums(d_value))

def reference(t_query, t_key, t_value, s_query, s_key, student_value, student_wo, projection, doc_ids, span_order):

    def per_sequence(running, items):
        seq_loss, d_weight, d_query, d_key, d_value = one_sequence(*items, student_wo, projection)
        return (running + d_weight, (seq_loss, d_query, d_key, d_value))
    start_weight = jnp.zeros((STUDENT_QUERIES * HEAD_WIDTH, DS), jnp.float32)
    d_wo, stacked = lax.scan(per_sequence, start_weight, (t_query, t_key, t_value, s_query, s_key, student_value, doc_ids, span_order))
    seq_loss, d_query, d_key, d_value = stacked
    return (seq_loss, d_wo, d_query, d_key, d_value)
```

```python
import functools
import math

import jax
import jax.numpy as jnp
from jax import lax
from jax.experimental import pallas as pl
from jax.experimental.pallas import tpu as pltpu
from jax.sharding import PartitionSpec as P

HEAD_WIDTH = 128
ROWS = 128
MASKED = -1e30
VMEM_LIMIT = 48 * 1024 * 1024
NT = (((1,), (1,)), ((), ()))
TN = (((0,), (0,)), ((), ()))


def windows(length):
    reach = length // 4
    out = []
    for first in range(0, length, ROWS):
        out.append((first, max(0, first - reach), first + ROWS))
    return out


def to_true_order(inverse_ref, source_ref, target_ref, halves, half):
    for place in range(halves):
        start = pl.multiple_of(inverse_ref[place] * half, half)
        target_ref[place * half : (place + 1) * half, :] = source_ref[pl.ds(start, half), :]


def block_weights(heads, queries, keys, doc_col, doc_row, first, low, high):
    scores = lax.dot_general(queries, keys, NT, preferred_element_type=jnp.float32)
    row_id = lax.broadcasted_iota(jnp.int32, (ROWS, high - low), 0) + first
    col_id = lax.broadcasted_iota(jnp.int32, (ROWS, high - low), 1) + low
    allowed = (doc_col == doc_row) & (col_id <= row_id)
    scores = scores.reshape(heads, ROWS, high - low)
    scores = jnp.where(allowed[None], scores, MASKED)
    top = jnp.max(scores, axis=2, keepdims=True)
    rate = 1.4426950408889634 / math.sqrt(HEAD_WIDTH)
    weights = jnp.exp2((scores - top) * rate)
    totals = jnp.sum(weights, axis=2, keepdims=True)
    return weights, totals


def stacked(ref, heads, first, last):
    return jnp.concatenate(
        [ref[first:last, h * HEAD_WIDTH : (h + 1) * HEAD_WIDTH] for h in range(heads)], axis=0
    )


def teacher_kernel(heads, halves, inverse_ref, pack_ref, col_ref, row_ref, out_ref, held):
    length = pack_ref.shape[0]
    to_true_order(inverse_ref, pack_ref, held, halves, length // halves)
    at = heads * HEAD_WIDTH
    for first, low, high in windows(length):
        queries = stacked(held, heads, first, first + ROWS)
        weights, totals = block_weights(
            heads, queries, held[low:high, at : at + HEAD_WIDTH],
            col_ref[first : first + ROWS, :], row_ref[:, low:high], first, low, high,
        )
        mixed = jnp.dot(
            weights.astype(jnp.bfloat16).reshape(heads * ROWS, high - low),
            held[low:high, at + HEAD_WIDTH : at + 2 * HEAD_WIDTH],
            preferred_element_type=jnp.float32,
        ).reshape(heads, ROWS, HEAD_WIDTH)
        mixed = (mixed / totals).astype(jnp.bfloat16)
        for h in range(heads):
            out_ref[first : first + ROWS, h * HEAD_WIDTH : (h + 1) * HEAD_WIDTH] = mixed[h]


def student_kernel(heads, halves, inverse_ref, pack_ref, col_ref, row_ref, out_ref, held, prob_ref):
    length = pack_ref.shape[0]
    to_true_order(inverse_ref, pack_ref, held, halves, length // halves)
    at = heads * HEAD_WIDTH
    for i, (first, low, high) in enumerate(windows(length)):
        queries = stacked(held, heads, first, first + ROWS)
        weights, totals = block_weights(
            heads, queries, held[low:high, at : at + HEAD_WIDTH],
            col_ref[first : first + ROWS, :], row_ref[:, low:high], first, low, high,
        )
        probs = (weights / totals).astype(jnp.bfloat16).reshape(heads * ROWS, high - low)
        prob_ref[i, :, : high - low] = probs
        mixed = jnp.dot(
            probs, held[low:high, at + HEAD_WIDTH : at + 2 * HEAD_WIDTH],
            preferred_element_type=jnp.float32,
        ).astype(jnp.bfloat16)
        for h in range(heads):
            out_ref[first : first + ROWS, h * HEAD_WIDTH : (h + 1) * HEAD_WIDTH] = mixed[
                h * ROWS : (h + 1) * ROWS
            ]


def back_kernel(heads, halves, order_ref, held_ref, prob_ref, so_ref, grad_ref, out_ref, done, dk, dv):
    length = held_ref.shape[0]
    half = length // halves
    at = heads * HEAD_WIDTH
    scaling = 1.0 / math.sqrt(HEAD_WIDTH)
    dk[...] = jnp.zeros_like(dk)
    dv[...] = jnp.zeros_like(dv)
    for i, (first, low, high) in enumerate(windows(length)):
        queries = stacked(held_ref, heads, first, first + ROWS)
        grads = stacked(grad_ref, heads, first, first + ROWS)
        outs = stacked(so_ref, heads, first, first + ROWS)
        probs = prob_ref[i, :, : high - low]
        delta = jnp.sum(
            grads.astype(jnp.float32) * outs.astype(jnp.float32), axis=1, keepdims=True
        )
        d_prob = lax.dot_general(
            grads, held_ref[low:high, at + HEAD_WIDTH : at + 2 * HEAD_WIDTH], NT,
            preferred_element_type=jnp.float32,
        )
        d_score = (probs.astype(jnp.float32) * (d_prob - delta)).astype(jnp.bfloat16)
        d_query = (
            jnp.dot(
                d_score, held_ref[low:high, at : at + HEAD_WIDTH],
                preferred_element_type=jnp.float32,
            )
            * scaling
        ).astype(jnp.bfloat16)
        for h in range(heads):
            done[first : first + ROWS, h * HEAD_WIDTH : (h + 1) * HEAD_WIDTH] = d_query[
                h * ROWS : (h + 1) * ROWS
            ]
        dk[low:high, :] += lax.dot_general(d_score, queries, TN, preferred_element_type=jnp.float32)
        dv[low:high, :] += lax.dot_general(probs, grads, TN, preferred_element_type=jnp.float32)
    done[:, at : at + HEAD_WIDTH] = (dk[...] * scaling).astype(jnp.bfloat16)
    done[:, at + HEAD_WIDTH : at + 2 * HEAD_WIDTH] = dv[...].astype(jnp.bfloat16)
    for place in range(halves):
        start = pl.multiple_of(order_ref[place] * half, half)
        out_ref[place * half : (place + 1) * half, :] = done[pl.ds(start, half), :]


SMEM = pl.BlockSpec(memory_space=pltpu.SMEM)
VMEM = pl.BlockSpec(memory_space=pltpu.VMEM)
PARAMS = pltpu.CompilerParams(vmem_limit_bytes=VMEM_LIMIT)


def shape(dims, dtype=jnp.bfloat16):
    return jax.ShapeDtypeStruct(dims, dtype)


def teacher_attention(heads, halves, inverse, pack, col, row):
    length, wide = pack.shape
    flops = 4 * heads * HEAD_WIDTH * length * (length // 4 + ROWS)
    return pl.pallas_call(
        functools.partial(teacher_kernel, heads, halves),
        out_shape=shape((length, heads * HEAD_WIDTH)),
        in_specs=[SMEM, VMEM, VMEM, VMEM],
        out_specs=VMEM,
        scratch_shapes=[pltpu.VMEM((length, wide), jnp.bfloat16)],
        compiler_params=PARAMS,
        cost_estimate=pl.CostEstimate(flops=flops, bytes_accessed=4 << 20, transcendentals=flops // 512),
        name="teacher_attention",
    )(inverse, pack, col, row)


def student_attention(heads, halves, inverse, pack, col, row):
    length, wide = pack.shape
    flops = 4 * heads * HEAD_WIDTH * length * (length // 4 + ROWS)
    return pl.pallas_call(
        functools.partial(student_kernel, heads, halves),
        out_shape=(
            shape((length, heads * HEAD_WIDTH)),
            shape((length, wide)),
            shape((length // ROWS, heads * ROWS, length // 4 + ROWS)),
        ),
        in_specs=[SMEM, VMEM, VMEM, VMEM],
        out_specs=(VMEM, VMEM, VMEM),
        compiler_params=PARAMS,
        cost_estimate=pl.CostEstimate(flops=flops, bytes_accessed=6 << 20, transcendentals=flops // 512),
        name="student_attention",
    )(inverse, pack, col, row)


def student_backward(heads, halves, order, held, probs, out, grad):
    length, wide = held.shape
    flops = 10 * heads * HEAD_WIDTH * length * (length // 4 + ROWS)
    return pl.pallas_call(
        functools.partial(back_kernel, heads, halves),
        out_shape=shape((length, wide)),
        in_specs=[SMEM, VMEM, VMEM, VMEM, VMEM],
        out_specs=VMEM,
        scratch_shapes=[
            pltpu.VMEM((length, wide), jnp.bfloat16),
            pltpu.VMEM((length, HEAD_WIDTH), jnp.float32),
            pltpu.VMEM((length, HEAD_WIDTH), jnp.float32),
        ],
        compiler_params=PARAMS,
        cost_estimate=pl.CostEstimate(flops=flops, bytes_accessed=6 << 20, transcendentals=0),
        name="student_backward",
    )(order, held, probs, out, grad)


def by_group(rows, groups):
    tokens, wide = rows.shape
    return jnp.transpose(rows.reshape(tokens, groups, wide // groups), (1, 0, 2))


def by_shared_head(rows, groups):
    heads = rows.shape[1] // HEAD_WIDTH
    return jnp.repeat(by_group(rows, heads), groups // heads, axis=0)


def shards(
    t_query,
    t_key,
    t_value,
    s_query,
    s_key,
    student_value,
    student_wo,
    projection,
    doc_ids,
    span_order,
):
    groups = lax.axis_size("seq")
    tokens = t_query.shape[1]
    length = tokens * groups
    halves = span_order.shape[1]
    t_local = t_query.shape[2] // HEAD_WIDTH // groups
    s_heads = s_query.shape[2] // HEAD_WIDTH
    s_local = s_heads // groups
    s_kv = s_key.shape[2] // HEAD_WIDTH
    order = span_order[0]
    places = jnp.arange(halves, dtype=jnp.int32)
    inverse = jnp.sum(
        jnp.where(order[None, :] == places[:, None], places[None, :], 0), axis=1, dtype=jnp.int32
    )
    col = doc_ids.reshape(length, 1)
    row = doc_ids.reshape(1, length)

    s_pack = jnp.concatenate(
        [
            by_group(s_query[0], groups),
            by_shared_head(s_key[0], groups),
            by_shared_head(student_value[0], groups),
        ],
        axis=2,
    )
    t_pack = jnp.concatenate(
        [
            by_group(t_query[0], groups),
            by_shared_head(t_key[0], groups),
            by_shared_head(t_value[0], groups),
        ],
        axis=2,
    )
    s_rows = lax.all_to_all(s_pack, "seq", split_axis=0, concat_axis=0, tiled=True)
    t_rows = lax.all_to_all(t_pack, "seq", split_axis=0, concat_axis=0, tiled=True)
    s_rows = s_rows.reshape(length, s_pack.shape[2])
    t_rows = t_rows.reshape(length, t_pack.shape[2])
    student_out, held, probs = student_attention(s_local, halves, inverse, s_rows, col, row)
    teacher_out = teacher_attention(t_local, halves, inverse, t_rows, col, row)

    width_all = student_wo.shape[1]
    own_diff = lax.psum_scatter(
        (
            jnp.dot(student_out, student_wo, preferred_element_type=jnp.float32)
            - jnp.dot(teacher_out, projection, preferred_element_type=jnp.float32)
        ).astype(jnp.bfloat16),
        "seq",
        scatter_dimension=0,
        tiled=True,
    )
    grad = lax.all_gather(own_diff, "seq", axis=0, tiled=True)
    grad32 = grad.astype(jnp.float32)
    seq_loss = (jnp.sum(grad32 * grad32) / (length * width_all)).reshape(1)
    d_weight = lax.dot_general(student_out, grad, TN, preferred_element_type=jnp.float32)
    weight_share = lax.psum_scatter(
        d_weight.astype(jnp.bfloat16), "rep", scatter_dimension=1, tiled=True
    ).astype(jnp.float32)
    d_attn = lax.dot_general(grad, student_wo, NT, preferred_element_type=jnp.float32).astype(
        jnp.bfloat16
    )
    back = student_backward(s_local, halves, order, held, probs, student_out, d_attn)
    back = lax.all_to_all(
        back.reshape(groups, tokens, back.shape[1]), "seq", split_axis=0, concat_axis=0, tiled=True
    )
    at = s_local * HEAD_WIDTH
    d_query = jnp.transpose(back[:, :, :at], (1, 0, 2)).reshape(1, tokens, s_heads * HEAD_WIDTH)

    def merge(parts):
        summed = parts.reshape(s_kv, groups // s_kv, tokens, HEAD_WIDTH).astype(jnp.float32)
        summed = summed.sum(axis=1).astype(jnp.bfloat16)
        return jnp.transpose(summed, (1, 0, 2)).reshape(1, tokens, s_kv * HEAD_WIDTH)

    return (
        seq_loss,
        weight_share,
        d_query,
        merge(back[:, :, at : at + HEAD_WIDTH]),
        merge(back[:, :, at + HEAD_WIDTH :]),
    )


def solution(mesh):
    in_specs = (
        P("rep", "seq", None),
        P("rep", "seq", None),
        P("rep", "seq", None),
        P("rep", "seq", None),
        P("rep", "seq", None),
        P("rep", "seq", None),
        P("seq", None),
        P("seq", None),
        P("rep", None),
        P("rep", None),
    )
    out_specs = (
        P("rep"),
        P("seq", "rep"),
        P("rep", "seq", None),
        P("rep", "seq", None),
        P("rep", "seq", None),
    )
    return jax.shard_map(shards, mesh=mesh, in_specs=in_specs, out_specs=out_specs, check_vma=False)
```

```python
import functools
import math

import jax
import jax.numpy as jnp
from jax import lax
from jax.experimental import pallas as pl
from jax.experimental.pallas import tpu as pltpu
from jax.sharding import PartitionSpec as P

HEAD_WIDTH = 128
ROWS = 128
CHUNKS = 8
MASKED = -1e30
VMEM_LIMIT = 48 * 1024 * 1024
NT = (((1,), (1,)), ((), ()))
TN = (((0,), (0,)), ((), ()))


def windows(length):
    reach = length // 4
    out = []
    for first in range(0, length, ROWS):
        out.append((first, max(0, first - reach), first + ROWS))
    return out


def to_true_order(inverse_ref, source_ref, target_ref, halves, half):
    for place in range(halves):
        start = pl.multiple_of(inverse_ref[place] * half, half)
        target_ref[place * half : (place + 1) * half, :] = source_ref[pl.ds(start, half), :]


def block_weights(heads, queries, keys, doc_col, doc_row, first, low, high):
    scores = lax.dot_general(queries, keys, NT, preferred_element_type=jnp.float32)
    row_id = lax.broadcasted_iota(jnp.int32, (ROWS, high - low), 0) + first
    col_id = lax.broadcasted_iota(jnp.int32, (ROWS, high - low), 1) + low
    allowed = (doc_col == doc_row) & (col_id <= row_id)
    scores = scores.reshape(heads, ROWS, high - low)
    scores = jnp.where(allowed[None], scores, MASKED)
    top = jnp.max(scores, axis=2, keepdims=True)
    rate = 1.4426950408889634 / math.sqrt(HEAD_WIDTH)
    weights = jnp.exp2((scores - top) * rate)
    totals = jnp.sum(weights, axis=2, keepdims=True)
    return weights, totals


def stacked(ref, heads, first, last):
    return jnp.concatenate(
        [ref[first:last, h * HEAD_WIDTH : (h + 1) * HEAD_WIDTH] for h in range(heads)], axis=0
    )


def teacher_kernel(heads, halves, inverse_ref, pack_ref, col_ref, row_ref, out_ref, held):
    length = pack_ref.shape[0]
    to_true_order(inverse_ref, pack_ref, held, halves, length // halves)
    at = heads * HEAD_WIDTH
    for first, low, high in windows(length):
        queries = stacked(held, heads, first, first + ROWS)
        weights, totals = block_weights(
            heads, queries, held[low:high, at : at + HEAD_WIDTH],
            col_ref[first : first + ROWS, :], row_ref[:, low:high], first, low, high,
        )
        mixed = jnp.dot(
            weights.astype(jnp.bfloat16).reshape(heads * ROWS, high - low),
            held[low:high, at + HEAD_WIDTH : at + 2 * HEAD_WIDTH],
            preferred_element_type=jnp.float32,
        ).reshape(heads, ROWS, HEAD_WIDTH)
        mixed = (mixed / totals).astype(jnp.bfloat16)
        for h in range(heads):
            out_ref[first : first + ROWS, h * HEAD_WIDTH : (h + 1) * HEAD_WIDTH] = mixed[h]


def student_kernel(heads, halves, inverse_ref, pack_ref, col_ref, row_ref, out_ref, held, prob_ref):
    length = pack_ref.shape[0]
    to_true_order(inverse_ref, pack_ref, held, halves, length // halves)
    at = heads * HEAD_WIDTH
    for i, (first, low, high) in enumerate(windows(length)):
        queries = stacked(held, heads, first, first + ROWS)
        weights, totals = block_weights(
            heads, queries, held[low:high, at : at + HEAD_WIDTH],
            col_ref[first : first + ROWS, :], row_ref[:, low:high], first, low, high,
        )
        probs = (weights / totals).astype(jnp.bfloat16).reshape(heads * ROWS, high - low)
        prob_ref[i, :, : high - low] = probs
        mixed = jnp.dot(
            probs, held[low:high, at + HEAD_WIDTH : at + 2 * HEAD_WIDTH],
            preferred_element_type=jnp.float32,
        ).astype(jnp.bfloat16)
        for h in range(heads):
            out_ref[first : first + ROWS, h * HEAD_WIDTH : (h + 1) * HEAD_WIDTH] = mixed[
                h * ROWS : (h + 1) * ROWS
            ]


def back_kernel(heads, halves, order_ref, held_ref, prob_ref, so_ref, grad_ref, out_ref, done, dk, dv):
    length = held_ref.shape[0]
    half = length // halves
    at = heads * HEAD_WIDTH
    scaling = 1.0 / math.sqrt(HEAD_WIDTH)
    dk[...] = jnp.zeros_like(dk)
    dv[...] = jnp.zeros_like(dv)
    for i, (first, low, high) in enumerate(windows(length)):
        queries = stacked(held_ref, heads, first, first + ROWS)
        grads = stacked(grad_ref, heads, first, first + ROWS)
        outs = stacked(so_ref, heads, first, first + ROWS)
        probs = prob_ref[i, :, : high - low]
        delta = jnp.sum(
            grads.astype(jnp.float32) * outs.astype(jnp.float32), axis=1, keepdims=True
        )
        d_prob = lax.dot_general(
            grads, held_ref[low:high, at + HEAD_WIDTH : at + 2 * HEAD_WIDTH], NT,
            preferred_element_type=jnp.float32,
        )
        d_score = (probs.astype(jnp.float32) * (d_prob - delta)).astype(jnp.bfloat16)
        d_query = (
            jnp.dot(
                d_score, held_ref[low:high, at : at + HEAD_WIDTH],
                preferred_element_type=jnp.float32,
            )
            * scaling
        ).astype(jnp.bfloat16)
        for h in range(heads):
            done[first : first + ROWS, h * HEAD_WIDTH : (h + 1) * HEAD_WIDTH] = d_query[
                h * ROWS : (h + 1) * ROWS
            ]
        dk[low:high, :] += lax.dot_general(d_score, queries, TN, preferred_element_type=jnp.float32)
        dv[low:high, :] += lax.dot_general(probs, grads, TN, preferred_element_type=jnp.float32)
    done[:, at : at + HEAD_WIDTH] = (dk[...] * scaling).astype(jnp.bfloat16)
    done[:, at + HEAD_WIDTH : at + 2 * HEAD_WIDTH] = dv[...].astype(jnp.bfloat16)
    for place in range(halves):
        start = pl.multiple_of(order_ref[place] * half, half)
        out_ref[place * half : (place + 1) * half, :] = done[pl.ds(start, half), :]


SMEM = pl.BlockSpec(memory_space=pltpu.SMEM)
VMEM = pl.BlockSpec(memory_space=pltpu.VMEM)
PARAMS = pltpu.CompilerParams(vmem_limit_bytes=VMEM_LIMIT)


def shape(dims, dtype=jnp.bfloat16):
    return jax.ShapeDtypeStruct(dims, dtype)


def teacher_attention(heads, halves, inverse, pack, col, row):
    length, wide = pack.shape
    flops = 4 * heads * HEAD_WIDTH * length * (length // 4 + ROWS)
    return pl.pallas_call(
        functools.partial(teacher_kernel, heads, halves),
        out_shape=shape((length, heads * HEAD_WIDTH)),
        in_specs=[SMEM, VMEM, VMEM, VMEM],
        out_specs=VMEM,
        scratch_shapes=[pltpu.VMEM((length, wide), jnp.bfloat16)],
        compiler_params=PARAMS,
        cost_estimate=pl.CostEstimate(flops=flops, bytes_accessed=4 << 20, transcendentals=flops // 512),
        name="teacher_attention",
    )(inverse, pack, col, row)


def student_attention(heads, halves, inverse, pack, col, row):
    length, wide = pack.shape
    flops = 4 * heads * HEAD_WIDTH * length * (length // 4 + ROWS)
    return pl.pallas_call(
        functools.partial(student_kernel, heads, halves),
        out_shape=(
            shape((length, heads * HEAD_WIDTH)),
            shape((length, wide)),
            shape((length // ROWS, heads * ROWS, length // 4 + ROWS)),
        ),
        in_specs=[SMEM, VMEM, VMEM, VMEM],
        out_specs=(VMEM, VMEM, VMEM),
        compiler_params=PARAMS,
        cost_estimate=pl.CostEstimate(flops=flops, bytes_accessed=6 << 20, transcendentals=flops // 512),
        name="student_attention",
    )(inverse, pack, col, row)


def student_backward(heads, halves, order, held, probs, out, grad):
    length, wide = held.shape
    flops = 10 * heads * HEAD_WIDTH * length * (length // 4 + ROWS)
    return pl.pallas_call(
        functools.partial(back_kernel, heads, halves),
        out_shape=shape((length, wide)),
        in_specs=[SMEM, VMEM, VMEM, VMEM, VMEM],
        out_specs=VMEM,
        scratch_shapes=[
            pltpu.VMEM((length, wide), jnp.bfloat16),
            pltpu.VMEM((length, HEAD_WIDTH), jnp.float32),
            pltpu.VMEM((length, HEAD_WIDTH), jnp.float32),
        ],
        compiler_params=PARAMS,
        cost_estimate=pl.CostEstimate(flops=flops, bytes_accessed=6 << 20, transcendentals=0),
        name="student_backward",
    )(order, held, probs, out, grad)


def exchange_kernel(
    chain, chunks, so_ref, to_ref, wo_ref, pj_ref, attn_ref, dw_ref, loss_ref,
    pair_out, pair_in, kept, far_out, far_in, grad, total,
    ps, pr, zs, zr, gs, gr, fs, fr,
):
    me = lax.axis_index("seq")
    mine, side = me // 2, me % 2
    other = 1 - side
    tokens = so_ref.shape[2]
    width = grad.shape[3]
    length = chain * 2 * tokens
    partner = {"seq": mine * 2 + other}
    peers = [lax.rem(mine + d, chain) for d in range(1, chain)]

    barrier = pltpu.get_barrier_semaphore()
    pl.semaphore_signal(barrier, inc=1, device_id=partner, device_id_type=pl.DeviceIdType.MESH)
    for peer in peers:
        pl.semaphore_signal(
            barrier, inc=1, device_id={"seq": peer * 2 + side}, device_id_type=pl.DeviceIdType.MESH
        )
    pl.semaphore_wait(barrier, chain)

    def copy(source, target, send, receive, device):
        return pltpu.make_async_remote_copy(
            src_ref=source, dst_ref=target, send_sem=send, recv_sem=receive,
            device_id=device, device_id_type=pl.DeviceIdType.MESH,
        )

    def pair_copy(c, t):
        return copy(pair_out.at[c, t], pair_in.at[c, t], ps.at[c, t], pr.at[c, t], partner)

    def far_copy(c, t):
        return copy(
            far_out.at[c, t], far_in.at[c, mine], zs.at[c, t], zr.at[c, mine], {"seq": t * 2 + side}
        )

    def far_arrival(c, t):
        return copy(
            far_out.at[c, t], far_in.at[c, t], zs.at[c, t], zr.at[c, t], {"seq": t * 2 + side}
        )

    def grad_copy(c, t):
        return copy(
            grad.at[c, me], grad.at[c, me], gs.at[c, t], gr.at[c, mine], {"seq": t * 2 + side}
        )

    def grad_arrival(c, t):
        block = grad.at[c, t * 2 + side]
        return copy(block, block, gs.at[c, t], gr.at[c, t], {"seq": t * 2 + side})

    def side_copy(c, t):
        block = grad.at[c, t * 2 + side]
        return copy(block, block, fs.at[c, t], fr.at[c, t], partner)

    def side_arrival(c, t):
        block = grad.at[c, t * 2 + other]
        return copy(block, block, fs.at[c, t], fr.at[c, t], partner)

    def partial(c, which):
        columns = slice(c * width, (c + 1) * width)
        rows = chain * tokens
        term = jnp.dot(
            so_ref[:, which].reshape(rows, so_ref.shape[3]), wo_ref[:, columns],
            preferred_element_type=jnp.float32,
        ) - jnp.dot(
            to_ref[:, which].reshape(rows, to_ref.shape[3]), pj_ref[:, columns],
            preferred_element_type=jnp.float32,
        )
        return term.astype(jnp.bfloat16).reshape(chain, tokens, width)

    def first_stage(c):
        pair_out[c] = partial(c, other)
        for t in range(chain):
            pair_copy(c, t).start()
        kept[c] = partial(c, side)

    def second_stage(c):
        for t in range(chain):
            pair_copy(c, t).wait_recv()
        far_out[c] = (kept[c].astype(jnp.float32) + pair_in[c].astype(jnp.float32)).astype(
            jnp.bfloat16
        )
        for peer in peers:
            far_copy(c, peer).start()

    def third_stage(c):
        summed = kept[c, mine].astype(jnp.float32) + pair_in[c, mine].astype(jnp.float32)
        for peer in peers:
            far_arrival(c, peer).wait_recv()
            summed = summed + far_in[c, peer].astype(jnp.float32)
        grad[c, me] = summed.astype(jnp.bfloat16)
        side_copy(c, mine).start()
        for peer in peers:
            grad_copy(c, peer).start()

    def fourth_stage(c):
        for peer in peers:
            grad_arrival(c, peer).wait_recv()
            side_copy(c, peer).start()

    def fifth_stage(c):
        for t in range(chain):
            side_arrival(c, t).wait_recv()
        columns = slice(c * width, (c + 1) * width)
        block = grad[c].reshape(length, width)
        wide = block.astype(jnp.float32)
        squares = jnp.sum(wide * wide, axis=0, keepdims=True)
        d_attn = lax.dot_general(block, wo_ref[:, columns], NT, preferred_element_type=jnp.float32)
        if c == 0:
            loss_ref[...] = squares
            total[...] = d_attn
        else:
            loss_ref[...] += squares
            total[...] += d_attn
        dw_ref[:, columns] = lax.dot_general(
            so_ref[...].reshape(length, so_ref.shape[3]), block, TN,
            preferred_element_type=jnp.float32,
        ).astype(jnp.bfloat16)

    stages = ((first_stage, 0), (second_stage, 2), (third_stage, 3), (fourth_stage, 4), (fifth_stage, 5))
    for step in range(chunks + 5):
        for stage, lag in stages:
            if 0 <= step - lag < chunks:
                stage(step - lag)
    attn_ref[...] = total[...].astype(jnp.bfloat16)
    for c in range(chunks):
        for t in range(chain):
            pair_copy(c, t).wait_send()
            side_copy(c, t).wait_send()
        for peer in peers:
            far_copy(c, peer).wait_send()
            grad_copy(c, peer).wait_send()


def exchange(groups, chunks, student_out, teacher_out, student_wo, projection):
    length, ws = student_out.shape
    wt = teacher_out.shape[1]
    chain, tokens = groups // 2, length // groups
    columns = student_wo.shape[1]
    width = columns // chunks
    block = (chunks, chain, tokens, width)
    sems = pltpu.SemaphoreType.DMA((chunks, chain))
    return pl.pallas_call(
        functools.partial(exchange_kernel, chain, chunks),
        out_shape=(
            shape((length, ws)), shape((ws, columns)), shape((1, width), jnp.float32),
        ),
        in_specs=[VMEM] * 4,
        out_specs=(VMEM, VMEM, VMEM),
        scratch_shapes=[pltpu.VMEM(block, jnp.bfloat16)] * 5
        + [
            pltpu.VMEM((chunks, groups, tokens, width), jnp.bfloat16),
            pltpu.VMEM((length, ws), jnp.float32),
        ]
        + [sems] * 8,
        compiler_params=pltpu.CompilerParams(
            collective_id=0, has_side_effects=True, vmem_limit_bytes=VMEM_LIMIT
        ),
        cost_estimate=pl.CostEstimate(
            flops=2 * length * columns * (3 * ws + wt), bytes_accessed=8 << 20, transcendentals=0
        ),
        name="exchange",
    )(
        student_out.reshape(chain, 2, tokens, ws), teacher_out.reshape(chain, 2, tokens, wt),
        student_wo, projection,
    )


def by_group(rows, groups):
    tokens, wide = rows.shape
    return jnp.transpose(rows.reshape(tokens, groups, wide // groups), (1, 0, 2))


def by_shared_head(rows, groups):
    heads = rows.shape[1] // HEAD_WIDTH
    return jnp.repeat(by_group(rows, heads), groups // heads, axis=0)


def shards(
    t_query,
    t_key,
    t_value,
    s_query,
    s_key,
    student_value,
    student_wo,
    projection,
    doc_ids,
    span_order,
):
    groups = lax.axis_size("seq")
    tokens = t_query.shape[1]
    length = tokens * groups
    halves = span_order.shape[1]
    t_local = t_query.shape[2] // HEAD_WIDTH // groups
    s_heads = s_query.shape[2] // HEAD_WIDTH
    s_local = s_heads // groups
    s_kv = s_key.shape[2] // HEAD_WIDTH
    order = span_order[0]
    places = jnp.arange(halves, dtype=jnp.int32)
    inverse = jnp.sum(
        jnp.where(order[None, :] == places[:, None], places[None, :], 0), axis=1, dtype=jnp.int32
    )
    col = doc_ids.reshape(length, 1)
    row = doc_ids.reshape(1, length)

    s_pack = jnp.concatenate(
        [
            by_group(s_query[0], groups),
            by_shared_head(s_key[0], groups),
            by_shared_head(student_value[0], groups),
        ],
        axis=2,
    )
    t_pack = jnp.concatenate(
        [
            by_group(t_query[0], groups),
            by_shared_head(t_key[0], groups),
            by_shared_head(t_value[0], groups),
        ],
        axis=2,
    )
    s_rows = lax.all_to_all(s_pack, "seq", split_axis=0, concat_axis=0, tiled=True)
    t_rows = lax.all_to_all(t_pack, "seq", split_axis=0, concat_axis=0, tiled=True)
    s_rows = s_rows.reshape(length, s_pack.shape[2])
    t_rows = t_rows.reshape(length, t_pack.shape[2])
    student_out, held, probs = student_attention(s_local, halves, inverse, s_rows, col, row)
    teacher_out = teacher_attention(t_local, halves, inverse, t_rows, col, row)

    width_all = student_wo.shape[1]
    d_attn, d_weight, squares = exchange(
        groups, CHUNKS, student_out, teacher_out, student_wo, projection
    )
    seq_loss = (jnp.sum(squares) / (length * width_all)).reshape(1)
    weight_share = lax.psum_scatter(
        d_weight, "rep", scatter_dimension=1, tiled=True
    ).astype(jnp.float32)
    back = student_backward(s_local, halves, order, held, probs, student_out, d_attn)
    back = lax.all_to_all(
        back.reshape(groups, tokens, back.shape[1]), "seq", split_axis=0, concat_axis=0, tiled=True
    )
    at = s_local * HEAD_WIDTH
    d_query = jnp.transpose(back[:, :, :at], (1, 0, 2)).reshape(1, tokens, s_heads * HEAD_WIDTH)

    def merge(parts):
        summed = parts.reshape(s_kv, groups // s_kv, tokens, HEAD_WIDTH).astype(jnp.float32)
        summed = summed.sum(axis=1).astype(jnp.bfloat16)
        return jnp.transpose(summed, (1, 0, 2)).reshape(1, tokens, s_kv * HEAD_WIDTH)

    return (
        seq_loss,
        weight_share,
        d_query,
        merge(back[:, :, at : at + HEAD_WIDTH]),
        merge(back[:, :, at + HEAD_WIDTH :]),
    )


def solution(mesh):
    in_specs = (
        P("rep", "seq", None),
        P("rep", "seq", None),
        P("rep", "seq", None),
        P("rep", "seq", None),
        P("rep", "seq", None),
        P("rep", "seq", None),
        P("seq", None),
        P("seq", None),
        P("rep", None),
        P("rep", None),
    )
    out_specs = (
        P("rep"),
        P("seq", "rep"),
        P("rep", "seq", None),
        P("rep", "seq", None),
        P("rep", "seq", None),
    )
    return jax.shard_map(shards, mesh=mesh, in_specs=in_specs, out_specs=out_specs, check_vma=False)
```

```python
import functools
import math

import jax
import jax.numpy as jnp
from jax import lax
from jax.experimental import pallas as pl
from jax.experimental.pallas import tpu as pltpu
from jax.sharding import PartitionSpec as P

HEAD_WIDTH = 128
ROWS = 128
PICKED = 256
CHUNKS = 16
MASKED = -1e30
VMEM_LIMIT = 48 * 1024 * 1024
NT = (((1,), (1,)), ((), ()))
TN = (((0,), (0,)), ((), ()))


def windows(length):
    reach = length // 4
    out = []
    for first in range(0, length, ROWS):
        out.append((first, max(0, first - reach), first + ROWS))
    return out


def block_weights(heads, queries, keys, doc_col, doc_row, first, low, high):
    scores = lax.dot_general(queries, keys, NT, preferred_element_type=jnp.float32)
    row_id = lax.broadcasted_iota(jnp.int32, (ROWS, high - low), 0) + first
    col_id = lax.broadcasted_iota(jnp.int32, (ROWS, high - low), 1) + low
    allowed = (doc_col == doc_row) & (col_id <= row_id)
    scores = scores.reshape(heads, ROWS, high - low)
    scores = jnp.where(allowed[None], scores, MASKED)
    top = jnp.max(scores, axis=2, keepdims=True)
    rate = 1.4426950408889634 / math.sqrt(HEAD_WIDTH)
    weights = jnp.exp2((scores - top) * rate)
    totals = jnp.sum(weights, axis=2, keepdims=True)
    return weights, totals


def stacked(ref, heads, first, last):
    return jnp.concatenate(
        [ref[first:last, h * HEAD_WIDTH : (h + 1) * HEAD_WIDTH] for h in range(heads)], axis=0
    )


def teacher_blocks(heads, held, col_ref, row_ref, out_ref):
    length = held.shape[0]
    at = heads * HEAD_WIDTH
    for first, low, high in windows(length):
        queries = stacked(held, heads, first, first + ROWS)
        weights, totals = block_weights(
            heads, queries, held[low:high, at : at + HEAD_WIDTH],
            col_ref[first : first + ROWS, :], row_ref[:, low:high], first, low, high,
        )
        mixed = jnp.dot(
            weights.astype(jnp.bfloat16).reshape(heads * ROWS, high - low),
            held[low:high, at + HEAD_WIDTH : at + 2 * HEAD_WIDTH],
            preferred_element_type=jnp.float32,
        ).reshape(heads, ROWS, HEAD_WIDTH)
        mixed = (mixed / totals).astype(jnp.bfloat16)
        for h in range(heads):
            out_ref[first : first + ROWS, h * HEAD_WIDTH : (h + 1) * HEAD_WIDTH] = mixed[h]


def student_blocks(heads, held, col_ref, row_ref, out_ref, prob_ref):
    length = held.shape[0]
    at = heads * HEAD_WIDTH
    for i, (first, low, high) in enumerate(windows(length)):
        queries = stacked(held, heads, first, first + ROWS)
        weights, totals = block_weights(
            heads, queries, held[low:high, at : at + HEAD_WIDTH],
            col_ref[first : first + ROWS, :], row_ref[:, low:high], first, low, high,
        )
        probs = (weights / totals).astype(jnp.bfloat16).reshape(heads * ROWS, high - low)
        prob_ref[i, :, : high - low] = probs
        mixed = jnp.dot(
            probs, held[low:high, at + HEAD_WIDTH : at + 2 * HEAD_WIDTH],
            preferred_element_type=jnp.float32,
        ).astype(jnp.bfloat16)
        for h in range(heads):
            out_ref[first : first + ROWS, h * HEAD_WIDTH : (h + 1) * HEAD_WIDTH] = mixed[
                h * ROWS : (h + 1) * ROWS
            ]


def reordered(source_rows, source):
    count, length = source_rows.shape[0], source.shape[0]
    places = lax.broadcasted_iota(jnp.int32, (count, length), 1)
    picks = jnp.where(source_rows == places, 1.0, 0.0).astype(jnp.bfloat16)
    return jnp.dot(picks, source, preferred_element_type=jnp.float32).astype(jnp.bfloat16)


MESH = pl.DeviceIdType.MESH


def greet(seq_peers, rep_peers=()):
    barrier = pltpu.get_barrier_semaphore()
    for peer in seq_peers:
        pl.semaphore_signal(barrier, inc=1, device_id={"seq": peer}, device_id_type=MESH)
    for peer in rep_peers:
        pl.semaphore_signal(barrier, inc=1, device_id={"rep": peer}, device_id_type=MESH)
    pl.semaphore_wait(barrier, len(seq_peers) + len(rep_peers))


def remote(source, target, send, receive, device):
    return pltpu.make_async_remote_copy(
        src_ref=source, dst_ref=target, send_sem=send, recv_sem=receive,
        device_id=device, device_id_type=MESH,
    )


def forward_kernel(
    groups, halves, inverse_ref, tq_ref, tk_ref, tv_ref, sq_ref, sk_ref, sv_ref, col_ref, row_ref,
    so_ref, held_ref, prob_ref, to_ref,
    sq_out, sq_in, tq_out, tq_in, kv_out, kv_in, t_held,
    sqs, sqr, tqs, tqr, kvs, kvr, fs, fr,
):
    me = lax.axis_index("seq")
    mine, side = me // 2, me % 2
    partner = mine * 2 + 1 - side
    chain, per = groups // 2, halves // groups
    half = sq_out.shape[2]
    ws, wt = sq_out.shape[3], tq_out.shape[3]
    kv_heads = kv_out.shape[0]
    share = groups // kv_heads
    everyone = [lax.rem(me + d, groups) for d in range(1, groups)]
    peers = [lax.rem(mine + d, chain) for d in range(1, chain)]
    greet(everyone)

    for j in range(kv_heads):
        columns = slice(j * HEAD_WIDTH, (j + 1) * HEAD_WIDTH)
        for n, ref in enumerate((sk_ref, sv_ref, tk_ref, tv_ref)):
            kv_out[j, :, :, n * HEAD_WIDTH : (n + 1) * HEAD_WIDTH] = ref[:, columns].reshape(
                per, half, HEAD_WIDTH
            )

    def slot(ref, g):
        return ref.at[pl.ds(g * per, per)]

    def kv_copy(t):
        head = t * 2 // share
        return remote(
            kv_out.at[head], slot(kv_in, me), kvs.at[t], kvr.at[mine], {"seq": t * 2 + side}
        )

    def kv_arrival(t):
        return remote(
            kv_out.at[0], slot(kv_in, t * 2 + side), kvs.at[t], kvr.at[t], {"seq": t * 2 + side}
        )

    def kv_forward(t):
        block = slot(kv_in, t * 2 + side)
        return remote(block, block, fs.at[t], fr.at[t], {"seq": partner})

    def kv_forwarded(t):
        block = slot(kv_in, t * 2 + 1 - side)
        return remote(block, block, fs.at[t], fr.at[t], {"seq": partner})

    def q_copy(out, into, send, receive, g):
        return remote(out.at[g], slot(into, me), send.at[g], receive.at[me], {"seq": g})

    def q_arrival(out, into, send, receive, g):
        return remote(out.at[g], slot(into, g), send.at[g], receive.at[g], {"seq": g})

    for t in peers:
        kv_copy(t).start()
    kv_in[pl.ds(me * per, per)] = kv_out[me // share]
    kv_forward(mine).start()
    for g in range(groups):
        sq_out[g] = sq_ref[:, g * ws : (g + 1) * ws].reshape(per, half, ws)
    for g in everyone:
        q_copy(sq_out, sq_in, sqs, sqr, g).start()
    sq_in[pl.ds(me * per, per)] = sq_out[me]
    for g in range(groups):
        tq_out[g] = tq_ref[:, g * wt : (g + 1) * wt].reshape(per, half, wt)
    for g in everyone:
        q_copy(tq_out, tq_in, tqs, tqr, g).start()
    tq_in[pl.ds(me * per, per)] = tq_out[me]
    for t in peers:
        kv_arrival(t).wait_recv()
        kv_forward(t).start()
    for t in range(chain):
        kv_forwarded(t).wait_recv()
    for g in everyone:
        q_arrival(sq_out, sq_in, sqs, sqr, g).wait_recv()
    length = halves * half
    queries = sq_in[...].reshape(length, ws)
    pairs = kv_in[...].reshape(length, 4 * HEAD_WIDTH)
    for at in range(0, length, PICKED):
        rows = slice(at, at + PICKED)
        held_ref[rows, :ws] = reordered(inverse_ref[rows, :], queries)
        moved = reordered(inverse_ref[rows, :], pairs)
        held_ref[rows, ws:] = moved[:, : 2 * HEAD_WIDTH]
        t_held[rows, wt:] = moved[:, 2 * HEAD_WIDTH :]
    student_blocks(ws // HEAD_WIDTH, held_ref, col_ref, row_ref, so_ref, prob_ref)
    for g in everyone:
        q_arrival(tq_out, tq_in, tqs, tqr, g).wait_recv()
    queries = tq_in[...].reshape(length, wt)
    for at in range(0, length, PICKED):
        rows = slice(at, at + PICKED)
        t_held[rows, :wt] = reordered(inverse_ref[rows, :], queries)
    teacher_blocks(wt // HEAD_WIDTH, t_held, col_ref, row_ref, to_ref)
    for t in peers:
        kv_copy(t).wait_send()
    for t in range(chain):
        kv_forward(t).wait_send()
    for g in everyone:
        q_copy(sq_out, sq_in, sqs, sqr, g).wait_send()
        q_copy(tq_out, tq_in, tqs, tqr, g).wait_send()


def back_kernel(
    groups, halves, reps, order_ref, held_ref, prob_ref, so_ref, grad_ref, dw_ref,
    dq_ref, dk_ref, dv_ref, dwo_ref,
    done, out, into, dw_in, dk, dv, qs, qr, ws_sem, wr_sem,
):
    me, rep = lax.axis_index("seq"), lax.axis_index("rep")
    length = held_ref.shape[0]
    half, per = length // halves, halves // groups
    tokens = per * half
    at = so_ref.shape[1]
    heads = at // HEAD_WIDTH
    scaling = 1.0 / math.sqrt(HEAD_WIDTH)
    everyone = [lax.rem(me + d, groups) for d in range(1, groups)]
    mates = [lax.rem(rep + d, reps) for d in range(1, reps)]
    greet(everyone, mates)

    def weight_copy(r):
        return remote(dw_ref.at[r], dw_in.at[rep], ws_sem.at[r], wr_sem.at[rep], {"rep": r})

    def weight_arrival(r):
        return remote(dw_ref.at[r], dw_in.at[r], ws_sem.at[r], wr_sem.at[r], {"rep": r})

    def copy(g):
        return remote(
            out.at[pl.ds(g * per, per)], into.at[me], qs.at[g], qr.at[me], {"seq": g}
        )

    def arrival(g):
        return remote(out.at[pl.ds(g * per, per)], into.at[g], qs.at[g], qr.at[g], {"seq": g})

    for r in mates:
        weight_copy(r).start()
    dk[...] = jnp.zeros_like(dk)
    dv[...] = jnp.zeros_like(dv)
    for i, (first, low, high) in enumerate(windows(length)):
        queries = stacked(held_ref, heads, first, first + ROWS)
        grads = stacked(grad_ref, heads, first, first + ROWS)
        outs = stacked(so_ref, heads, first, first + ROWS)
        probs = prob_ref[i, :, : high - low]
        delta = jnp.sum(
            grads.astype(jnp.float32) * outs.astype(jnp.float32), axis=1, keepdims=True
        )
        d_prob = lax.dot_general(
            grads, held_ref[low:high, at + HEAD_WIDTH : at + 2 * HEAD_WIDTH], NT,
            preferred_element_type=jnp.float32,
        )
        d_score = (probs.astype(jnp.float32) * (d_prob - delta)).astype(jnp.bfloat16)
        d_query = (
            jnp.dot(
                d_score, held_ref[low:high, at : at + HEAD_WIDTH],
                preferred_element_type=jnp.float32,
            )
            * scaling
        ).astype(jnp.bfloat16)
        for h in range(heads):
            done[first : first + ROWS, h * HEAD_WIDTH : (h + 1) * HEAD_WIDTH] = d_query[
                h * ROWS : (h + 1) * ROWS
            ]
        dk[low:high, :] += lax.dot_general(d_score, queries, TN, preferred_element_type=jnp.float32)
        dv[low:high, :] += lax.dot_general(probs, grads, TN, preferred_element_type=jnp.float32)
    done[:, at : at + HEAD_WIDTH] = (dk[...] * scaling).astype(jnp.bfloat16)
    done[:, at + HEAD_WIDTH : at + 2 * HEAD_WIDTH] = dv[...].astype(jnp.bfloat16)
    everything = done[...]
    count = PICKED // half
    for top in range(0, length, PICKED):
        moved = reordered(order_ref[top : top + PICKED, :], everything)
        out[top // half : top // half + count] = moved.reshape(count, half, moved.shape[1])
    for g in everyone:
        copy(g).start()
    into[me] = out[pl.ds(me * per, per)]
    for r in mates:
        weight_arrival(r).wait_recv()
    total = dw_ref[rep].astype(jnp.float32)
    for r in mates:
        total = total + dw_in[r].astype(jnp.float32)
    dwo_ref[...] = total
    for g in everyone:
        arrival(g).wait_recv()
    for g in range(groups):
        dq_ref[:, g * at : (g + 1) * at] = into[g, :, :, :at].reshape(tokens, at)
    kv_heads = dk_ref.shape[1] // HEAD_WIDTH
    share = groups // kv_heads
    for j in range(kv_heads):
        both = into[j * share, :, :, at:].astype(jnp.float32)
        for g in range(j * share + 1, (j + 1) * share):
            both = both + into[g, :, :, at:].astype(jnp.float32)
        both = both.astype(jnp.bfloat16).reshape(tokens, 2 * HEAD_WIDTH)
        dk_ref[:, j * HEAD_WIDTH : (j + 1) * HEAD_WIDTH] = both[:, :HEAD_WIDTH]
        dv_ref[:, j * HEAD_WIDTH : (j + 1) * HEAD_WIDTH] = both[:, HEAD_WIDTH:]
    for r in mates:
        weight_copy(r).wait_send()
    for g in everyone:
        copy(g).wait_send()


VMEM = pl.BlockSpec(memory_space=pltpu.VMEM)


def remote_params(number):
    return pltpu.CompilerParams(
        collective_id=number, has_side_effects=True, vmem_limit_bytes=VMEM_LIMIT
    )


def shape(dims, dtype=jnp.bfloat16):
    return jax.ShapeDtypeStruct(dims, dtype)


def forward(groups, halves, inverse, t_query, t_key, t_value, s_query, s_key, s_value, col, row):
    length = col.shape[0]
    tokens = t_query.shape[0]
    half, per = length // halves, halves // groups
    ws, wt = s_query.shape[1] // groups, t_query.shape[1] // groups
    kv_heads = s_key.shape[1] // HEAD_WIDTH
    flops = 4 * (ws + wt) * length * (length // 4 + ROWS)
    bf16 = jnp.bfloat16
    sems = pltpu.SemaphoreType.DMA
    return pl.pallas_call(
        functools.partial(forward_kernel, groups, halves),
        out_shape=(
            shape((length, ws)),
            shape((length, ws + 2 * HEAD_WIDTH)),
            shape((length // ROWS, ws // HEAD_WIDTH * ROWS, length // 4 + ROWS)),
            shape((length, wt)),
        ),
        in_specs=[VMEM] * 9,
        out_specs=(VMEM,) * 4,
        scratch_shapes=[
            pltpu.VMEM((groups, per, half, ws), bf16),
            pltpu.VMEM((halves, half, ws), bf16),
            pltpu.VMEM((groups, per, half, wt), bf16),
            pltpu.VMEM((halves, half, wt), bf16),
            pltpu.VMEM((kv_heads, per, half, 4 * HEAD_WIDTH), bf16),
            pltpu.VMEM((halves, half, 4 * HEAD_WIDTH), bf16),
            pltpu.VMEM((length, wt + 2 * HEAD_WIDTH), bf16),
        ]
        + [sems((groups,))] * 4
        + [sems((groups // 2,))] * 4,
        compiler_params=remote_params(1),
        cost_estimate=pl.CostEstimate(flops=flops, bytes_accessed=6 << 20, transcendentals=flops // 512),
        name="forward",
    )(inverse, t_query, t_key, t_value, s_query, s_key, s_value, col, row)


def backward(groups, halves, order, held, probs, out, grad, d_weight, kv_columns):
    length, wide = held.shape
    half, per, tokens = length // halves, halves // groups, length // groups
    ws = out.shape[1]
    reps, _, columns = d_weight.shape
    flops = 10 * ws * length * (length // 4 + ROWS)
    bf16 = jnp.bfloat16
    sems = pltpu.SemaphoreType.DMA
    return pl.pallas_call(
        functools.partial(back_kernel, groups, halves, reps),
        out_shape=(
            shape((tokens, ws * groups)),
            shape((tokens, kv_columns)),
            shape((tokens, kv_columns)),
            shape((ws, columns), jnp.float32),
        ),
        in_specs=[VMEM] * 6,
        out_specs=(VMEM,) * 4,
        scratch_shapes=[
            pltpu.VMEM((length, wide), bf16),
            pltpu.VMEM((halves, half, wide), bf16),
            pltpu.VMEM((groups, per, half, wide), bf16),
            pltpu.VMEM((reps, ws, columns), bf16),
            pltpu.VMEM((length, HEAD_WIDTH), jnp.float32),
            pltpu.VMEM((length, HEAD_WIDTH), jnp.float32),
            sems((groups,)), sems((groups,)), sems((reps,)), sems((reps,)),
        ],
        compiler_params=remote_params(2),
        cost_estimate=pl.CostEstimate(flops=flops, bytes_accessed=6 << 20, transcendentals=0),
        name="backward",
    )(order, held, probs, out, grad, d_weight)


def exchange_kernel(
    chain, chunks, so_ref, to_ref, wo_ref, pj_ref, attn_ref, dw_ref, loss_ref,
    pair_out, pair_in, kept, far_out, far_in, grad, total,
    ps, pr, zs, zr, gs, gr, fs, fr,
):
    me = lax.axis_index("seq")
    mine, side = me // 2, me % 2
    other = 1 - side
    tokens = so_ref.shape[2]
    width = grad.shape[3]
    length = chain * 2 * tokens
    partner = {"seq": mine * 2 + other}
    peers = [lax.rem(mine + d, chain) for d in range(1, chain)]

    greet([mine * 2 + other] + [peer * 2 + side for peer in peers])
    copy = remote

    def pair_copy(c, t):
        return copy(pair_out.at[c, t], pair_in.at[c, t], ps.at[c, t], pr.at[c, t], partner)

    def far_copy(c, t):
        return copy(
            far_out.at[c, t], far_in.at[c, mine], zs.at[c, t], zr.at[c, mine], {"seq": t * 2 + side}
        )

    def far_arrival(c, t):
        return copy(
            far_out.at[c, t], far_in.at[c, t], zs.at[c, t], zr.at[c, t], {"seq": t * 2 + side}
        )

    def grad_copy(c, t):
        return copy(
            grad.at[c, me], grad.at[c, me], gs.at[c, t], gr.at[c, mine], {"seq": t * 2 + side}
        )

    def grad_arrival(c, t):
        block = grad.at[c, t * 2 + side]
        return copy(block, block, gs.at[c, t], gr.at[c, t], {"seq": t * 2 + side})

    def side_copy(c, t):
        block = grad.at[c, t * 2 + side]
        return copy(block, block, fs.at[c, t], fr.at[c, t], partner)

    def side_arrival(c, t):
        block = grad.at[c, t * 2 + other]
        return copy(block, block, fs.at[c, t], fr.at[c, t], partner)

    def partial(c, which):
        columns = slice(c * width, (c + 1) * width)
        rows = chain * tokens
        term = jnp.dot(
            so_ref[:, which].reshape(rows, so_ref.shape[3]), wo_ref[:, columns],
            preferred_element_type=jnp.float32,
        ) - jnp.dot(
            to_ref[:, which].reshape(rows, to_ref.shape[3]), pj_ref[:, columns],
            preferred_element_type=jnp.float32,
        )
        return term.astype(jnp.bfloat16).reshape(chain, tokens, width)

    def first_stage(c):
        pair_out[c] = partial(c, other)
        for t in range(chain):
            pair_copy(c, t).start()
        kept[c] = partial(c, side)

    def second_stage(c):
        for t in range(chain):
            pair_copy(c, t).wait_recv()
        far_out[c] = (kept[c].astype(jnp.float32) + pair_in[c].astype(jnp.float32)).astype(
            jnp.bfloat16
        )
        for peer in peers:
            far_copy(c, peer).start()

    def third_stage(c):
        summed = kept[c, mine].astype(jnp.float32) + pair_in[c, mine].astype(jnp.float32)
        for peer in peers:
            far_arrival(c, peer).wait_recv()
            summed = summed + far_in[c, peer].astype(jnp.float32)
        grad[c, me] = summed.astype(jnp.bfloat16)
        side_copy(c, mine).start()
        for peer in peers:
            grad_copy(c, peer).start()

    def fourth_stage(c):
        for peer in peers:
            grad_arrival(c, peer).wait_recv()
            side_copy(c, peer).start()

    def fifth_stage(c):
        for t in range(chain):
            side_arrival(c, t).wait_recv()
        columns = slice(c * width, (c + 1) * width)
        block = grad[c].reshape(length, width)
        wide = block.astype(jnp.float32)
        squares = jnp.sum(wide * wide, axis=0, keepdims=True)
        d_attn = lax.dot_general(block, wo_ref[:, columns], NT, preferred_element_type=jnp.float32)
        if c == 0:
            loss_ref[...] = squares
            total[...] = d_attn
        else:
            loss_ref[...] += squares
            total[...] += d_attn
        share = dw_ref.shape[2]
        at = c * width % share
        dw_ref[c * width // share, :, at : at + width] = lax.dot_general(
            so_ref[...].reshape(length, so_ref.shape[3]), block, TN,
            preferred_element_type=jnp.float32,
        ).astype(jnp.bfloat16)

    stages = ((first_stage, 0), (second_stage, 2), (third_stage, 3), (fourth_stage, 4), (fifth_stage, 5))
    for step in range(chunks + 5):
        for stage, lag in stages:
            if 0 <= step - lag < chunks:
                stage(step - lag)
    attn_ref[...] = total[...].astype(jnp.bfloat16)
    for c in range(chunks):
        for t in range(chain):
            pair_copy(c, t).wait_send()
            side_copy(c, t).wait_send()
        for peer in peers:
            far_copy(c, peer).wait_send()
            grad_copy(c, peer).wait_send()


def exchange(groups, reps, chunks, student_out, teacher_out, student_wo, projection):
    length, ws = student_out.shape
    wt = teacher_out.shape[1]
    chain, tokens = groups // 2, length // groups
    columns = student_wo.shape[1]
    width = columns // chunks
    block = (chunks, chain, tokens, width)
    sems = pltpu.SemaphoreType.DMA((chunks, chain))
    return pl.pallas_call(
        functools.partial(exchange_kernel, chain, chunks),
        out_shape=(
            shape((length, ws)), shape((reps, ws, columns // reps)),
            shape((1, width), jnp.float32),
        ),
        in_specs=[VMEM] * 4,
        out_specs=(VMEM, VMEM, VMEM),
        scratch_shapes=[pltpu.VMEM(block, jnp.bfloat16)] * 5
        + [
            pltpu.VMEM((chunks, groups, tokens, width), jnp.bfloat16),
            pltpu.VMEM((length, ws), jnp.float32),
        ]
        + [sems] * 8,
        compiler_params=remote_params(0),
        cost_estimate=pl.CostEstimate(
            flops=2 * length * columns * (3 * ws + wt), bytes_accessed=8 << 20, transcendentals=0
        ),
        name="exchange",
    )(
        student_out.reshape(chain, 2, tokens, ws), teacher_out.reshape(chain, 2, tokens, wt),
        student_wo, projection,
    )


def shards(
    t_query,
    t_key,
    t_value,
    s_query,
    s_key,
    student_value,
    student_wo,
    projection,
    doc_ids,
    span_order,
):
    groups, reps = lax.axis_size("seq"), lax.axis_size("rep")
    length = t_query.shape[1] * groups
    halves = span_order.shape[1]
    order = span_order[0]
    places = jnp.arange(halves, dtype=jnp.int32)
    inverse = jnp.sum(
        jnp.where(order[None, :] == places[:, None], places[None, :], 0), axis=1, dtype=jnp.int32
    )
    half = length // halves
    offsets = jnp.arange(half, dtype=jnp.int32)
    inverse = (inverse[:, None] * half + offsets[None, :]).reshape(length, 1)
    order = (order[:, None] * half + offsets[None, :]).reshape(length, 1)
    student_out, held, probs, teacher_out = forward(
        groups, halves, inverse, t_query[0], t_key[0], t_value[0], s_query[0], s_key[0], student_value[0],
        doc_ids.reshape(length, 1), doc_ids.reshape(1, length),
    )
    d_attn, d_weight, squares = exchange(
        groups, reps, CHUNKS, student_out, teacher_out, student_wo, projection
    )
    seq_loss = (jnp.sum(squares) / (length * student_wo.shape[1])).reshape(1)
    d_query, d_key, d_value, d_wo = backward(
        groups, halves, order, held, probs, student_out, d_attn, d_weight, s_key.shape[2]
    )
    return (seq_loss, d_wo, d_query[None], d_key[None], d_value[None])


def solution(mesh):
    in_specs = (
        P("rep", "seq", None),
        P("rep", "seq", None),
        P("rep", "seq", None),
        P("rep", "seq", None),
        P("rep", "seq", None),
        P("rep", "seq", None),
        P("seq", None),
        P("seq", None),
        P("rep", None),
        P("rep", None),
    )
    out_specs = (
        P("rep"),
        P("seq", "rep"),
        P("rep", "seq", None),
        P("rep", "seq", None),
        P("rep", "seq", None),
    )
    return jax.shard_map(shards, mesh=mesh, in_specs=in_specs, out_specs=out_specs, check_vma=False)
```

```python
import functools
import math

import jax
import jax.numpy as jnp
from jax import lax
from jax.experimental import pallas as pl
from jax.experimental.pallas import tpu as pltpu
from jax.sharding import PartitionSpec as P

HEAD_WIDTH = 128
ROWS = 128
PICKED = 256
CHUNKS = 16
MASKED = -1e30
VMEM_LIMIT = 48 * 1024 * 1024
FORWARD_LIMIT = 62 * 1024 * 1024
NT = (((1,), (1,)), ((), ()))
TN = (((0,), (0,)), ((), ()))


def windows(length):
    reach = length // 4
    out = []
    for first in range(0, length, ROWS):
        out.append((first, max(0, first - reach), first + ROWS))
    return out


def block_weights(heads, queries, keys, doc_col, doc_row, first, low, high):
    scores = lax.dot_general(queries, keys, NT, preferred_element_type=jnp.float32)
    row_id = lax.broadcasted_iota(jnp.int32, (ROWS, high - low), 0) + first
    col_id = lax.broadcasted_iota(jnp.int32, (ROWS, high - low), 1) + low
    allowed = (doc_col == doc_row) & (col_id <= row_id)
    scores = scores.reshape(heads, ROWS, high - low)
    scores = jnp.where(allowed[None], scores, MASKED)
    top = jnp.max(scores, axis=2, keepdims=True)
    rate = 1.4426950408889634 / math.sqrt(HEAD_WIDTH)
    weights = jnp.exp2((scores - top) * rate)
    totals = jnp.sum(weights, axis=2, keepdims=True)
    return weights, totals


def stacked(ref, heads, first, last):
    return jnp.concatenate(
        [ref[first:last, h * HEAD_WIDTH : (h + 1) * HEAD_WIDTH] for h in range(heads)], axis=0
    )


def teacher_blocks(heads, held, col_ref, row_ref, out_ref):
    length = held.shape[0]
    at = heads * HEAD_WIDTH
    for first, low, high in windows(length):
        queries = stacked(held, heads, first, first + ROWS)
        weights, totals = block_weights(
            heads, queries, held[low:high, at : at + HEAD_WIDTH],
            col_ref[first : first + ROWS, :], row_ref[:, low:high], first, low, high,
        )
        mixed = jnp.dot(
            weights.astype(jnp.bfloat16).reshape(heads * ROWS, high - low),
            held[low:high, at + HEAD_WIDTH : at + 2 * HEAD_WIDTH],
            preferred_element_type=jnp.float32,
        ).reshape(heads, ROWS, HEAD_WIDTH)
        mixed = (mixed / totals).astype(jnp.bfloat16)
        for h in range(heads):
            out_ref[first : first + ROWS, h * HEAD_WIDTH : (h + 1) * HEAD_WIDTH] = mixed[h]


def student_blocks(heads, held, col_ref, row_ref, out_ref, prob_ref):
    length = held.shape[0]
    at = heads * HEAD_WIDTH
    for i, (first, low, high) in enumerate(windows(length)):
        queries = stacked(held, heads, first, first + ROWS)
        weights, totals = block_weights(
            heads, queries, held[low:high, at : at + HEAD_WIDTH],
            col_ref[first : first + ROWS, :], row_ref[:, low:high], first, low, high,
        )
        probs = (weights / totals).astype(jnp.bfloat16).reshape(heads * ROWS, high - low)
        prob_ref[i, :, : high - low] = probs
        mixed = jnp.dot(
            probs, held[low:high, at + HEAD_WIDTH : at + 2 * HEAD_WIDTH],
            preferred_element_type=jnp.float32,
        ).astype(jnp.bfloat16)
        for h in range(heads):
            out_ref[first : first + ROWS, h * HEAD_WIDTH : (h + 1) * HEAD_WIDTH] = mixed[
                h * ROWS : (h + 1) * ROWS
            ]


def reordered(spans_ref, top, half, source):
    length = source.shape[0]
    offset = lax.broadcasted_iota(jnp.int32, (half, length), 1) - lax.broadcasted_iota(
        jnp.int32, (half, length), 0
    )
    picks = jnp.concatenate(
        [
            jnp.where(offset == spans_ref[place] * half, 1.0, 0.0).astype(jnp.bfloat16)
            for place in range(top // half, (top + PICKED) // half)
        ],
        axis=0,
    )
    return jnp.dot(picks, source, preferred_element_type=jnp.float32).astype(jnp.bfloat16)


MESH = pl.DeviceIdType.MESH


def greet(seq_peers, rep_peers=()):
    barrier = pltpu.get_barrier_semaphore()
    for peer in seq_peers:
        pl.semaphore_signal(barrier, inc=1, device_id={"seq": peer}, device_id_type=MESH)
    for peer in rep_peers:
        pl.semaphore_signal(barrier, inc=1, device_id={"rep": peer}, device_id_type=MESH)
    pl.semaphore_wait(barrier, len(seq_peers) + len(rep_peers))


def remote(source, target, send, receive, device):
    return pltpu.make_async_remote_copy(
        src_ref=source, dst_ref=target, send_sem=send, recv_sem=receive,
        device_id=device, device_id_type=MESH,
    )


def forward_kernel(
    groups, halves, inverse_ref, tq_hbm, tk_hbm, tv_hbm, sq_hbm, sk_hbm, sv_hbm, col_ref, row_ref,
    so_ref, held_ref, prob_ref, to_ref,
    tq_ref, tk_ref, tv_ref, sq_ref, sk_ref, sv_ref, local,
    sq_out, sq_in, tq_out, tq_in, kv_out, kv_in, t_held,
    sqs, sqr, tqs, tqr, kvs, kvr, fs, fr,
):
    me = lax.axis_index("seq")
    mine, side = me // 2, me % 2
    partner = mine * 2 + 1 - side
    chain, per = groups // 2, halves // groups
    half = sq_out.shape[2]
    ws, wt = sq_out.shape[3], tq_out.shape[3]
    kv_heads = kv_out.shape[0]
    share = groups // kv_heads
    everyone = [lax.rem(me + d, groups) for d in range(1, groups)]
    peers = [lax.rem(mine + d, chain) for d in range(1, chain)]
    loads = [
        pltpu.make_async_copy(source, target, local.at[n])
        for n, (source, target) in enumerate(
            (
                (sk_hbm, sk_ref), (sv_hbm, sv_ref), (tk_hbm, tk_ref), (tv_hbm, tv_ref),
                (sq_hbm, sq_ref), (tq_hbm, tq_ref),
            )
        )
    ]
    for load in loads:
        load.start()
    greet(everyone)

    for load in loads:
        load.wait()
    for j in range(kv_heads):
        columns = slice(j * HEAD_WIDTH, (j + 1) * HEAD_WIDTH)
        for n, ref in enumerate((sk_ref, sv_ref, tk_ref, tv_ref)):
            kv_out[j, :, :, n * HEAD_WIDTH : (n + 1) * HEAD_WIDTH] = ref[:, columns].reshape(
                per, half, HEAD_WIDTH
            )

    def slot(ref, g):
        return ref.at[pl.ds(g * per, per)]

    def kv_copy(t):
        head = t * 2 // share
        return remote(
            kv_out.at[head], slot(kv_in, me), kvs.at[t], kvr.at[mine], {"seq": t * 2 + side}
        )

    def kv_arrival(t):
        return remote(
            kv_out.at[0], slot(kv_in, t * 2 + side), kvs.at[t], kvr.at[t], {"seq": t * 2 + side}
        )

    def kv_forward(t):
        block = slot(kv_in, t * 2 + side)
        return remote(block, block, fs.at[t], fr.at[t], {"seq": partner})

    def kv_forwarded(t):
        block = slot(kv_in, t * 2 + 1 - side)
        return remote(block, block, fs.at[t], fr.at[t], {"seq": partner})

    def q_copy(out, into, send, receive, g):
        return remote(out.at[g], slot(into, me), send.at[g], receive.at[me], {"seq": g})

    def q_arrival(out, into, send, receive, g):
        return remote(out.at[g], slot(into, g), send.at[g], receive.at[g], {"seq": g})

    for t in peers:
        kv_copy(t).start()
    kv_in[pl.ds(me * per, per)] = kv_out[me // share]
    kv_forward(mine).start()
    for g in range(groups):
        sq_out[g] = sq_ref[:, g * ws : (g + 1) * ws].reshape(per, half, ws)
    for g in everyone:
        q_copy(sq_out, sq_in, sqs, sqr, g).start()
    sq_in[pl.ds(me * per, per)] = sq_out[me]
    for g in range(groups):
        tq_out[g] = tq_ref[:, g * wt : (g + 1) * wt].reshape(per, half, wt)
    for g in everyone:
        q_copy(tq_out, tq_in, tqs, tqr, g).start()
    tq_in[pl.ds(me * per, per)] = tq_out[me]
    for t in peers:
        kv_arrival(t).wait_recv()
        kv_forward(t).start()
    for t in range(chain):
        kv_forwarded(t).wait_recv()
    for g in everyone:
        q_arrival(sq_out, sq_in, sqs, sqr, g).wait_recv()
    length = halves * half
    queries = sq_in[...].reshape(length, ws)
    pairs = kv_in[...].reshape(length, 4 * HEAD_WIDTH)
    for at in range(0, length, PICKED):
        rows = slice(at, at + PICKED)
        held_ref[rows, :ws] = reordered(inverse_ref, at, half, queries)
        moved = reordered(inverse_ref, at, half, pairs)
        held_ref[rows, ws:] = moved[:, : 2 * HEAD_WIDTH]
        t_held[rows, wt:] = moved[:, 2 * HEAD_WIDTH :]
    student_blocks(ws // HEAD_WIDTH, held_ref, col_ref, row_ref, so_ref, prob_ref)
    for g in everyone:
        q_arrival(tq_out, tq_in, tqs, tqr, g).wait_recv()
    queries = tq_in[...].reshape(length, wt)
    for at in range(0, length, PICKED):
        rows = slice(at, at + PICKED)
        t_held[rows, :wt] = reordered(inverse_ref, at, half, queries)
    teacher_blocks(wt // HEAD_WIDTH, t_held, col_ref, row_ref, to_ref)
    for t in peers:
        kv_copy(t).wait_send()
    for t in range(chain):
        kv_forward(t).wait_send()
    for g in everyone:
        q_copy(sq_out, sq_in, sqs, sqr, g).wait_send()
        q_copy(tq_out, tq_in, tqs, tqr, g).wait_send()


def back_kernel(
    groups, halves, reps, order_ref, held_ref, prob_ref, so_ref, grad_ref, dw_ref,
    dq_ref, dk_ref, dv_ref, dwo_ref,
    done, out, into, dw_in, dk, dv, qs, qr, ws_sem, wr_sem,
):
    me, rep = lax.axis_index("seq"), lax.axis_index("rep")
    length = held_ref.shape[0]
    half, per = length // halves, halves // groups
    tokens = per * half
    at = so_ref.shape[1]
    heads = at // HEAD_WIDTH
    scaling = 1.0 / math.sqrt(HEAD_WIDTH)
    everyone = [lax.rem(me + d, groups) for d in range(1, groups)]
    mates = [lax.rem(rep + d, reps) for d in range(1, reps)]
    greet(everyone, mates)

    def weight_copy(r):
        return remote(dw_ref.at[r], dw_in.at[rep], ws_sem.at[r], wr_sem.at[rep], {"rep": r})

    def weight_arrival(r):
        return remote(dw_ref.at[r], dw_in.at[r], ws_sem.at[r], wr_sem.at[r], {"rep": r})

    def copy(g):
        return remote(
            out.at[pl.ds(g * per, per)], into.at[me], qs.at[g], qr.at[me], {"seq": g}
        )

    def arrival(g):
        return remote(out.at[pl.ds(g * per, per)], into.at[g], qs.at[g], qr.at[g], {"seq": g})

    for r in mates:
        weight_copy(r).start()
    dk[...] = jnp.zeros_like(dk)
    dv[...] = jnp.zeros_like(dv)
    for i, (first, low, high) in enumerate(windows(length)):
        queries = stacked(held_ref, heads, first, first + ROWS)
        grads = stacked(grad_ref, heads, first, first + ROWS)
        outs = stacked(so_ref, heads, first, first + ROWS)
        probs = prob_ref[i, :, : high - low]
        delta = jnp.sum(
            grads.astype(jnp.float32) * outs.astype(jnp.float32), axis=1, keepdims=True
        )
        d_prob = lax.dot_general(
            grads, held_ref[low:high, at + HEAD_WIDTH : at + 2 * HEAD_WIDTH], NT,
            preferred_element_type=jnp.float32,
        )
        d_score = (probs.astype(jnp.float32) * (d_prob - delta)).astype(jnp.bfloat16)
        d_query = (
            jnp.dot(
                d_score, held_ref[low:high, at : at + HEAD_WIDTH],
                preferred_element_type=jnp.float32,
            )
            * scaling
        ).astype(jnp.bfloat16)
        for h in range(heads):
            done[first : first + ROWS, h * HEAD_WIDTH : (h + 1) * HEAD_WIDTH] = d_query[
                h * ROWS : (h + 1) * ROWS
            ]
        dk[low:high, :] += lax.dot_general(d_score, queries, TN, preferred_element_type=jnp.float32)
        dv[low:high, :] += lax.dot_general(probs, grads, TN, preferred_element_type=jnp.float32)
    done[:, at : at + HEAD_WIDTH] = (dk[...] * scaling).astype(jnp.bfloat16)
    done[:, at + HEAD_WIDTH : at + 2 * HEAD_WIDTH] = dv[...].astype(jnp.bfloat16)
    everything = done[...]
    count = PICKED // half
    for top in range(0, length, PICKED):
        moved = reordered(order_ref, top, half, everything)
        out[top // half : top // half + count] = moved.reshape(count, half, moved.shape[1])
    for g in everyone:
        copy(g).start()
    into[me] = out[pl.ds(me * per, per)]
    for r in mates:
        weight_arrival(r).wait_recv()
    total = dw_ref[rep].astype(jnp.float32)
    for r in mates:
        total = total + dw_in[r].astype(jnp.float32)
    dwo_ref[...] = total
    for g in everyone:
        arrival(g).wait_recv()
    for g in range(groups):
        dq_ref[:, g * at : (g + 1) * at] = into[g, :, :, :at].reshape(tokens, at)
    kv_heads = dk_ref.shape[1] // HEAD_WIDTH
    share = groups // kv_heads
    for j in range(kv_heads):
        both = into[j * share, :, :, at:].astype(jnp.float32)
        for g in range(j * share + 1, (j + 1) * share):
            both = both + into[g, :, :, at:].astype(jnp.float32)
        both = both.astype(jnp.bfloat16).reshape(tokens, 2 * HEAD_WIDTH)
        dk_ref[:, j * HEAD_WIDTH : (j + 1) * HEAD_WIDTH] = both[:, :HEAD_WIDTH]
        dv_ref[:, j * HEAD_WIDTH : (j + 1) * HEAD_WIDTH] = both[:, HEAD_WIDTH:]
    for r in mates:
        weight_copy(r).wait_send()
    for g in everyone:
        copy(g).wait_send()


SMEM = pl.BlockSpec(memory_space=pltpu.SMEM)
VMEM = pl.BlockSpec(memory_space=pltpu.VMEM)


def remote_params(number, limit=VMEM_LIMIT):
    return pltpu.CompilerParams(
        collective_id=number, has_side_effects=True, vmem_limit_bytes=limit
    )


def shape(dims, dtype=jnp.bfloat16):
    return jax.ShapeDtypeStruct(dims, dtype)


def forward(groups, halves, inverse, t_query, t_key, t_value, s_query, s_key, s_value, col, row):
    length = col.shape[0]
    tokens = t_query.shape[0]
    half, per = length // halves, halves // groups
    ws, wt = s_query.shape[1] // groups, t_query.shape[1] // groups
    kv_heads = s_key.shape[1] // HEAD_WIDTH
    flops = 4 * (ws + wt) * length * (length // 4 + ROWS)
    bf16 = jnp.bfloat16
    sems = pltpu.SemaphoreType.DMA
    return pl.pallas_call(
        functools.partial(forward_kernel, groups, halves),
        out_shape=(
            shape((length, ws)),
            shape((length, ws + 2 * HEAD_WIDTH)),
            shape((length // ROWS, ws // HEAD_WIDTH * ROWS, length // 4 + ROWS)),
            shape((length, wt)),
        ),
        in_specs=[SMEM] + [pl.BlockSpec(memory_space=pltpu.HBM)] * 6 + [VMEM] * 2,
        out_specs=(VMEM,) * 4,
        scratch_shapes=[
            pltpu.VMEM(array.shape, bf16)
            for array in (t_query, t_key, t_value, s_query, s_key, s_value)
        ]
        + [
            sems((6,)),
            pltpu.VMEM((groups, per, half, ws), bf16),
            pltpu.VMEM((halves, half, ws), bf16),
            pltpu.VMEM((groups, per, half, wt), bf16),
            pltpu.VMEM((halves, half, wt), bf16),
            pltpu.VMEM((kv_heads, per, half, 4 * HEAD_WIDTH), bf16),
            pltpu.VMEM((halves, half, 4 * HEAD_WIDTH), bf16),
            pltpu.VMEM((length, wt + 2 * HEAD_WIDTH), bf16),
        ]
        + [sems((groups,))] * 4
        + [sems((groups // 2,))] * 4,
        compiler_params=remote_params(1, FORWARD_LIMIT),
        cost_estimate=pl.CostEstimate(flops=flops, bytes_accessed=6 << 20, transcendentals=flops // 512),
        name="forward",
    )(inverse, t_query, t_key, t_value, s_query, s_key, s_value, col, row)


def backward(groups, halves, order, held, probs, out, grad, d_weight, kv_columns):
    length, wide = held.shape
    half, per, tokens = length // halves, halves // groups, length // groups
    ws = out.shape[1]
    reps, _, columns = d_weight.shape
    flops = 10 * ws * length * (length // 4 + ROWS)
    bf16 = jnp.bfloat16
    sems = pltpu.SemaphoreType.DMA
    return pl.pallas_call(
        functools.partial(back_kernel, groups, halves, reps),
        out_shape=(
            shape((tokens, ws * groups)),
            shape((tokens, kv_columns)),
            shape((tokens, kv_columns)),
            shape((ws, columns), jnp.float32),
        ),
        in_specs=[SMEM] + [VMEM] * 5,
        out_specs=(VMEM,) * 4,
        scratch_shapes=[
            pltpu.VMEM((length, wide), bf16),
            pltpu.VMEM((halves, half, wide), bf16),
            pltpu.VMEM((groups, per, half, wide), bf16),
            pltpu.VMEM((reps, ws, columns), bf16),
            pltpu.VMEM((length, HEAD_WIDTH), jnp.float32),
            pltpu.VMEM((length, HEAD_WIDTH), jnp.float32),
            sems((groups,)), sems((groups,)), sems((reps,)), sems((reps,)),
        ],
        compiler_params=remote_params(2),
        cost_estimate=pl.CostEstimate(flops=flops, bytes_accessed=6 << 20, transcendentals=0),
        name="backward",
    )(order, held, probs, out, grad, d_weight)


def exchange_kernel(
    chain, chunks, so_ref, to_ref, wo_ref, pj_ref, attn_ref, dw_ref, loss_ref,
    pair_out, pair_in, kept, far_out, far_in, grad, total,
    ps, pr, zs, zr, gs, gr, fs, fr,
):
    me = lax.axis_index("seq")
    mine, side = me // 2, me % 2
    other = 1 - side
    tokens = so_ref.shape[2]
    width = grad.shape[3]
    length = chain * 2 * tokens
    partner = {"seq": mine * 2 + other}
    peers = [lax.rem(mine + d, chain) for d in range(1, chain)]

    greet([mine * 2 + other] + [peer * 2 + side for peer in peers])
    copy = remote

    def pair_copy(c, t):
        return copy(pair_out.at[c, t], pair_in.at[c, t], ps.at[c, t], pr.at[c, t], partner)

    def far_copy(c, t):
        return copy(
            far_out.at[c, t], far_in.at[c, mine], zs.at[c, t], zr.at[c, mine], {"seq": t * 2 + side}
        )

    def far_arrival(c, t):
        return copy(
            far_out.at[c, t], far_in.at[c, t], zs.at[c, t], zr.at[c, t], {"seq": t * 2 + side}
        )

    def grad_copy(c, t):
        return copy(
            grad.at[c, me], grad.at[c, me], gs.at[c, t], gr.at[c, mine], {"seq": t * 2 + side}
        )

    def grad_arrival(c, t):
        block = grad.at[c, t * 2 + side]
        return copy(block, block, gs.at[c, t], gr.at[c, t], {"seq": t * 2 + side})

    def side_copy(c, t):
        block = grad.at[c, t * 2 + side]
        return copy(block, block, fs.at[c, t], fr.at[c, t], partner)

    def side_arrival(c, t):
        block = grad.at[c, t * 2 + other]
        return copy(block, block, fs.at[c, t], fr.at[c, t], partner)

    def partial(c, which):
        columns = slice(c * width, (c + 1) * width)
        rows = chain * tokens
        term = jnp.dot(
            so_ref[:, which].reshape(rows, so_ref.shape[3]), wo_ref[:, columns],
            preferred_element_type=jnp.float32,
        ) - jnp.dot(
            to_ref[:, which].reshape(rows, to_ref.shape[3]), pj_ref[:, columns],
            preferred_element_type=jnp.float32,
        )
        return term.astype(jnp.bfloat16).reshape(chain, tokens, width)

    def first_stage(c):
        pair_out[c] = partial(c, other)
        for t in range(chain):
            pair_copy(c, t).start()
        kept[c] = partial(c, side)

    def second_stage(c):
        for t in range(chain):
            pair_copy(c, t).wait_recv()
        far_out[c] = (kept[c].astype(jnp.float32) + pair_in[c].astype(jnp.float32)).astype(
            jnp.bfloat16
        )
        for peer in peers:
            far_copy(c, peer).start()

    def third_stage(c):
        summed = kept[c, mine].astype(jnp.float32) + pair_in[c, mine].astype(jnp.float32)
        for peer in peers:
            far_arrival(c, peer).wait_recv()
            summed = summed + far_in[c, peer].astype(jnp.float32)
        grad[c, me] = summed.astype(jnp.bfloat16)
        side_copy(c, mine).start()
        for peer in peers:
            grad_copy(c, peer).start()

    def fourth_stage(c):
        for peer in peers:
            grad_arrival(c, peer).wait_recv()
            side_copy(c, peer).start()

    def fifth_stage(c):
        for t in range(chain):
            side_arrival(c, t).wait_recv()
        columns = slice(c * width, (c + 1) * width)
        block = grad[c].reshape(length, width)
        wide = block.astype(jnp.float32)
        squares = jnp.sum(wide * wide, axis=0, keepdims=True)
        d_attn = lax.dot_general(block, wo_ref[:, columns], NT, preferred_element_type=jnp.float32)
        if c == 0:
            loss_ref[...] = squares
            total[...] = d_attn
        else:
            loss_ref[...] += squares
            total[...] += d_attn
        share = dw_ref.shape[2]
        at = c * width % share
        dw_ref[c * width // share, :, at : at + width] = lax.dot_general(
            so_ref[...].reshape(length, so_ref.shape[3]), block, TN,
            preferred_element_type=jnp.float32,
        ).astype(jnp.bfloat16)

    stages = ((first_stage, 0), (second_stage, 3), (third_stage, 4), (fourth_stage, 5), (fifth_stage, 7))
    for step in range(chunks + 7):
        for stage, lag in stages:
            if 0 <= step - lag < chunks:
                stage(step - lag)
    attn_ref[...] = total[...].astype(jnp.bfloat16)
    for c in range(chunks):
        for t in range(chain):
            pair_copy(c, t).wait_send()
            side_copy(c, t).wait_send()
        for peer in peers:
            far_copy(c, peer).wait_send()
            grad_copy(c, peer).wait_send()


def exchange(groups, reps, chunks, student_out, teacher_out, student_wo, projection):
    length, ws = student_out.shape
    wt = teacher_out.shape[1]
    chain, tokens = groups // 2, length // groups
    columns = student_wo.shape[1]
    width = columns // chunks
    block = (chunks, chain, tokens, width)
    sems = pltpu.SemaphoreType.DMA((chunks, chain))
    return pl.pallas_call(
        functools.partial(exchange_kernel, chain, chunks),
        out_shape=(
            shape((length, ws)), shape((reps, ws, columns // reps)),
            shape((1, width), jnp.float32),
        ),
        in_specs=[VMEM] * 4,
        out_specs=(VMEM, VMEM, VMEM),
        scratch_shapes=[pltpu.VMEM(block, jnp.bfloat16)] * 5
        + [
            pltpu.VMEM((chunks, groups, tokens, width), jnp.bfloat16),
            pltpu.VMEM((length, ws), jnp.float32),
        ]
        + [sems] * 8,
        compiler_params=remote_params(0),
        cost_estimate=pl.CostEstimate(
            flops=2 * length * columns * (3 * ws + wt), bytes_accessed=8 << 20, transcendentals=0
        ),
        name="exchange",
    )(
        student_out.reshape(chain, 2, tokens, ws), teacher_out.reshape(chain, 2, tokens, wt),
        student_wo, projection,
    )


def shards(
    t_query,
    t_key,
    t_value,
    s_query,
    s_key,
    student_value,
    student_wo,
    projection,
    doc_ids,
    span_order,
):
    groups, reps = lax.axis_size("seq"), lax.axis_size("rep")
    length = t_query.shape[1] * groups
    halves = span_order.shape[1]
    order = span_order[0]
    places = jnp.arange(halves, dtype=jnp.int32)
    inverse = jnp.sum(
        jnp.where(order[None, :] == places[:, None], places[None, :], 0), axis=1, dtype=jnp.int32
    )
    student_out, held, probs, teacher_out = forward(
        groups, halves, inverse, t_query[0], t_key[0], t_value[0], s_query[0], s_key[0], student_value[0],
        doc_ids.reshape(length, 1), doc_ids.reshape(1, length),
    )
    d_attn, d_weight, squares = exchange(
        groups, reps, CHUNKS, student_out, teacher_out, student_wo, projection
    )
    seq_loss = (jnp.sum(squares) / (length * student_wo.shape[1])).reshape(1)
    d_query, d_key, d_value, d_wo = backward(
        groups, halves, order, held, probs, student_out, d_attn, d_weight, s_key.shape[2]
    )
    return (seq_loss, d_wo, d_query[None], d_key[None], d_value[None])


def solution(mesh):
    in_specs = (
        P("rep", "seq", None),
        P("rep", "seq", None),
        P("rep", "seq", None),
        P("rep", "seq", None),
        P("rep", "seq", None),
        P("rep", "seq", None),
        P("seq", None),
        P("seq", None),
        P("rep", None),
        P("rep", None),
    )
    out_specs = (
        P("rep"),
        P("seq", "rep"),
        P("rep", "seq", None),
        P("rep", "seq", None),
        P("rep", "seq", None),
    )
    return jax.shard_map(shards, mesh=mesh, in_specs=in_specs, out_specs=out_specs, check_vma=False)
```
